32 devices in a mesh: groups: 2 (over y), tensor: 4 (over z), expert: 4 (over x, core).
Axes of the slice: x: 2, y: 2, z: 4, core: 2. Of those that a mesh axis runs over, the one named last changes fastest.
Arguments:
- hidden_in: bfloat16 [64, 4096], P(('groups', 'expert'), 'tensor'), parts along dimension 0, may hold values from -6 to 6
- queries: bfloat16 [64, 4096], P(('groups', 'expert')), parts along dimension 0, may hold values from -140 to 140
- cache_keys: bfloat16 [64, 1024, 512], P(('groups', 'expert'), 'tensor'), parts along dimension 0, may hold values from -4 to 4
- cache_values: bfloat16 [64, 1024, 512], P(('groups', 'expert'), 'tensor'), parts along dimension 0, may hold values from -6 to 6
- new_key: bfloat16 [64, 512], P(('groups', 'expert')), parts along dimension 0, may hold values from -6 to 6
- new_value: bfloat16 [64, 512], P(('groups', 'expert')), parts along dimension 0, may hold values from -6 to 6
- cache_lengths: int32 [64], P(('groups', 'expert')), parts along dimension 0, may hold values from 2 to 1024, as said below
- out_weight: bfloat16 [4096, 4096], P('tensor'), may hold values from -2 to 2
- norm_gain: bfloat16 [4096], P('tensor'), may hold values from 0.5 to 1.5
- gate_probs: float32 [64, 8], P(('groups', 'expert')), parts along dimension 0, may hold values from 0.05 to 1
- expert_ids: int32 [64, 8], P(('groups', 'expert')), parts along dimension 0, may hold values from 0 to 63, all different within a row; in each aligned block of 8 rows (0 to 7, 8 to 15, ...) at most 2 rows name the same one
- gate_up: bfloat16 [64, 4096, 1536], P('expert', 'tensor'), may hold values from -0.09375 to 0.09375
- down_proj: bfloat16 [64, 768, 4096], P('expert', None, 'tensor'), may hold values from -0.21875 to 0.21875
Outputs:
- mixed: bfloat16 [64, 4096], P(('groups', 'expert'), 'tensor'), parts along dimension 0
The draws below stay inside these ranges and needn't reach their ends.
There are 2 independent parts, one for each index of `groups`. The reference program is written for one: setup_inputs(seed, part) draws one part's arguments, and reference() takes and returns one part's arrays. A program takes and returns all parts, laid end to end along the dimension named above; an argument that names none is the same for every part. Nothing has to cross between parts.
Inputs may be any that keep to these rules, and one draw needn't show every extreme that they name: Positions below cache_lengths[r] of row r are live; some row has 1024 live positions. `expert_ids`: each row names 8 different experts; among the rows of one index of expert (aligned blocks of 8 rows) no expert is named more than 2 times, and in some block one expert is named exactly 2 times.
All inputs are finite; a program needn't handle non-finite values.
Results may differ from the reference program's by a relative error of at most 0.023.
Values may be sent and summed in bfloat16 or wider, within the bound.
A program may use at most 192 MiB of HBM per device.

```python
import math
import jax
import jax.numpy as jnp
import numpy as np
from jax import lax

D = 4096
HD = 128
KV = 4
TOP = 8
HQ = 32
FF = 768
EXPERTS = 64
CACHE = 1024
ROWS_DEV = 8
ROWS = 32
HEADS_DEV = 8
MOST = 2
N_TENSOR = 4


def shared_cache(key):
    values = jax.random.normal(key, (ROWS, CACHE, KV * HD), jnp.float32)
    return jnp.clip(values, -4.0, 4.0)


def wild_rows():
    return (jnp.arange(ROWS) % 4 == 1)[:, None]


def draw_cache_keys(key, part):
    base_keys = shared_cache(key)
    damped = jnp.where(wild_rows()[:, :, None], 0.25 * base_keys, base_keys)
    return damped.astype(jnp.bfloat16)


def draw_queries(key, part):
    key = jax.random.fold_in(key, 5)
    wild = jax.random.uniform(jax.random.fold_in(key, 17), (ROWS, HQ * HD), jnp.float32, -100.0, 100.0)
    result = jnp.clip(jax.random.normal(key, (ROWS, HQ * HD), jnp.float32), -4.0, 4.0)
    result = jnp.where(wild_rows(), wild, result)
    return result.astype(jnp.bfloat16)


def draw_cache_lengths(key, part):
    key = jax.random.fold_in(key, 7)
    lengths = jax.random.randint(key, (ROWS,), 2, CACHE + 1, jnp.int32)
    lengths = lengths.at[0].set(CACHE)
    return lengths.at[ROWS - 1].set(2)


def draw_hidden_in(key, part):
    key = jax.random.fold_in(key, 11)
    entry_key, scale_key = jax.random.split(key)
    base = jnp.clip(jax.random.normal(entry_key, (ROWS, D), jnp.float32), -6.0, 6.0)
    exponent = jax.random.uniform(scale_key, (ROWS,), jnp.float32, -1.7, 0.0)
    row_scale = jnp.exp(exponent * math.log(10.0))
    return (base * row_scale[:, None]).astype(jnp.bfloat16)


def draw_out_weight(key, part):
    key = jax.random.fold_in(key, 13)
    entry_key, rough_key, pair_key = jax.random.split(key, 3)
    block_count = HQ // HEADS_DEV
    feature = jnp.arange(D, dtype=jnp.float32) / D
    base = jnp.clip(jax.random.normal(entry_key, (HQ * HD, D), jnp.float32), -6.0, 6.0)
    column = jnp.exp((feature - 0.5) * math.log(10.0))
    rough = jax.random.uniform(rough_key, (D,), jnp.float32, 0.5, 1.5)
    pairing = jax.random.permutation(pair_key, block_count)
    row_block = jnp.arange(HQ * HD) // (HEADS_DEV * HD)
    col_block = jnp.arange(D) // (D // block_count)
    spike = jnp.where(pairing[row_block][:, None] == col_block[None, :], 3.0, 1.0)
    values = base * (1.0 / math.sqrt(HQ * HD)) * (column * rough)[None, :] * spike
    return jnp.clip(values, -2.0, 2.0).astype(jnp.bfloat16)


def block_levels(stream_key, extent, cuts, least, high):
    def one(position, parts):
        draws = jax.random.uniform(jax.random.fold_in(jax.random.fold_in(stream_key, 6), position), (parts,), jnp.float32, least / len(cuts), high / len(cuts))
        return jnp.repeat(jnp.exp(draws), extent[position] // parts).reshape((-1,) + (1,) * (len(extent) - position - 1))

    loudness = one(*cuts[0])
    for cut in cuts[1:]:
        loudness = loudness * one(*cut)
    return loudness


def deal_out(key, own, number, rows, number_of, top, bound, lean):
    sequence = jax.random.permutation(key, number_of)
    crowded, common = shares(number_of, rows * top, bound, lean, True), shares(number_of, rows * top, bound, lean, False)
    places = jnp.arange(number_of)

    def named(sizes, rotation):
        used = int((sizes > 0).sum())
        fixed = max(1, used // 4)
        moved = fixed + (places - fixed + rotation * (used - fixed)) % max(1, number_of - fixed)
        return jnp.zeros((number_of,), jnp.int32).at[sequence[jnp.where(places < fixed, places, moved)]].set(jnp.asarray(sizes, jnp.int32))

    sizes = jnp.where(number % 4 == 0, named(crowded, number // 4), named(common, number - number // 4 - 1))
    mixed = jax.random.permutation(jax.random.fold_in(own, 3), number_of)
    giver, receiver = mixed[0:number_of // 2 * 2:2], mixed[1:number_of // 2 * 2:2]
    room = jnp.minimum(sizes[giver] - 1, bound - sizes[receiver]) // 2
    room = jnp.where((giver == sequence[0]) | (receiver == sequence[0]) | (sizes[receiver] == 0), 0, jnp.maximum(room, 0))
    moved = jax.random.randint(jax.random.fold_in(own, 4), (number_of // 2,), 0, 1 << 20) % (room + 1)
    sizes = sizes.at[giver].add(-moved).at[receiver].add(moved)
    items = jnp.searchsorted(jnp.cumsum(sizes), jnp.arange(rows * top), side="right").astype(jnp.int32)
    table = items.reshape(top, rows).T
    table = table[jax.random.permutation(jax.random.fold_in(own, 1), rows)]
    rotation = jax.random.randint(jax.random.fold_in(own, 2), (rows, 1), 0, top)
    return jnp.take_along_axis(table, (jnp.arange(top)[None, :] + rotation) % top, axis=1)


def shares(amount, total, limit, slope, full):
    weights = [(1 << 20) // math.isqrt(standing ** slope) + 1 for standing in range(1, amount + 1)]
    largest = limit if full else min(limit, max(-(-total // amount), total * weights[0] // sum(weights)))
    least = 1 if total - largest >= amount - 1 else 0
    holding, rest = [largest] + [least] * (amount - 1), total - largest - least * (amount - 1)
    while rest > 0:
        movable = [i for i in range(1, amount) if holding[i] < largest] or [i for i in range(1, amount) if holding[i] < limit]
        pool, left = sum([weights[i] for i in movable]), rest
        for i in movable:
            addition = min(limit - holding[i], max(1, left * weights[i] // pool), rest)
            holding[i] = holding[i] + addition
            rest = rest - addition
    return np.array(holding)


def scatter_about(stream_key, extent, width, limit, pieces=(), kind=jnp.bfloat16):
    array = jax.random.normal(stream_key, extent, jnp.float32) * width
    if len(pieces) > 0:
        array = block_levels(stream_key, extent, pieces, -0.22, 0.18) * array
    return jnp.clip(array, min=-limit, max=limit).astype(kind)


def setup_inputs(seed: int = 0, part: int = 0) -> dict:
    splits = jax.random.split(jax.random.key(seed), 14)
    own_keys = jax.random.split(jax.random.fold_in(splits[13], part), 14)
    hidden_in = draw_hidden_in(jax.random.fold_in(jax.random.fold_in(splits[13], part), 71), part)
    queries = draw_queries(jax.random.fold_in(jax.random.fold_in(splits[13], part), 71), part)
    cache_keys = draw_cache_keys(jax.random.fold_in(jax.random.fold_in(splits[13], part), 71), part)
    cache_values = scatter_about(own_keys[3], (ROWS, CACHE, KV * HD), 1.0, 6.0, ((0, 4), (1, 4)))
    new_key = scatter_about(own_keys[4], (ROWS, KV * HD), 1.0, 6.0, ((0, 4),))
    new_value = scatter_about(own_keys[5], (ROWS, KV * HD), 1.0, 6.0, ((0, 4),))
    cache_lengths = draw_cache_lengths(jax.random.fold_in(jax.random.fold_in(splits[13], part), 71), part)
    out_weight = draw_out_weight(jax.random.fold_in(splits[13], 71), part)
    norm_gain = jnp.clip(1.0 + 0.1 * jax.random.normal(splits[8], (D,), jnp.float32), 0.5, 1.5).astype(jnp.bfloat16)
    gate_probs = jnp.clip(0.05 + 0.95 * jax.random.uniform(own_keys[9], (ROWS, TOP), jnp.float32) ** block_levels(own_keys[9], (ROWS, TOP), ((0, 4),), -0.2, 0.2), 0.05, 1.0)
    expert_ids_keys = jax.random.split(jax.random.fold_in(own_keys[10], 1), ROWS // ROWS_DEV)
    expert_ids_turns = jax.random.permutation(jax.random.fold_in(own_keys[10], 3), ROWS // ROWS_DEV)
    expert_ids = jax.vmap(lambda own, number: deal_out(jax.random.fold_in(own_keys[10], 2), own, number, ROWS_DEV, EXPERTS, TOP, MOST, 2))(expert_ids_keys, expert_ids_turns).reshape((ROWS, TOP))
    gate_up = scatter_about(splits[11], (EXPERTS, D, 2 * FF), D ** -0.5, 0.09375, ((0, 4), (1, 4)))
    down_proj = scatter_about(splits[12], (EXPERTS, FF, D), FF ** -0.5, 0.21875, ((0, 4), (2, 4)))
    return {"hidden_in": hidden_in, "queries": queries, "cache_keys": cache_keys, "cache_values": cache_values, "new_key": new_key, "new_value": new_value, "cache_lengths": cache_lengths, "out_weight": out_weight, "norm_gain": norm_gain, "gate_probs": gate_probs, "expert_ids": expert_ids, "gate_up": gate_up, "down_proj": down_proj}


neg_large = -1e+30

def reference(hidden_in, queries, cache_keys, cache_values, new_key, new_value, cache_lengths, out_weight, norm_gain, gate_probs, expert_ids, gate_up, down_proj):
    group_size = HQ // KV
    score_scale = 1.0 / math.sqrt(HD)
    query_heads = queries.astype(jnp.float32).reshape(ROWS, KV, group_size, HD)
    key_heads = cache_keys.astype(jnp.float32).reshape(ROWS, CACHE, KV, HD)
    value_heads = cache_values.astype(jnp.float32).reshape(ROWS, CACHE, KV, HD)
    scores = jnp.einsum('rkgd,rpkd->rkgp', query_heads, key_heads) * score_scale
    live_mask = (jnp.arange(CACHE, dtype=jnp.int32)[None, :] < cache_lengths[:, None])[:, None, None, :]
    own_score = jnp.einsum('rkgd,rkd->rkg', query_heads, new_key.astype(jnp.float32).reshape(ROWS, KV, HD)) * score_scale
    highest = jnp.maximum(lax.optimization_barrier(jnp.max(jnp.where(live_mask, scores, neg_large), axis=3)), own_score)
    weights = jnp.where(live_mask, jnp.exp(scores - highest[..., None]), 0.0)
    own_weight = jnp.exp(own_score - highest)
    totals = lax.optimization_barrier(jnp.sum(weights, axis=3)) + own_weight
    low_weights = lax.optimization_barrier(weights.astype(jnp.bfloat16)).astype(jnp.float32)
    low_own = lax.optimization_barrier(own_weight.astype(jnp.bfloat16)).astype(jnp.float32)
    numerator = jnp.einsum('rkgp,rpkd->rkgd', low_weights, value_heads)
    numerator = numerator + low_own[..., None] * new_value.astype(jnp.float32).reshape(ROWS, KV, 1, HD)
    attended = (numerator / totals[..., None]).astype(jnp.bfloat16)
    attended = attended.reshape(ROWS, N_TENSOR, HEADS_DEV * HD).astype(jnp.float32)
    proj_parts = jnp.einsum('rtk,tkd->rtd', attended, out_weight.astype(jnp.float32).reshape(N_TENSOR, HEADS_DEV * HD, D))
    proj_sum = lax.optimization_barrier(jnp.sum(lax.optimization_barrier(proj_parts.astype(jnp.bfloat16)).astype(jnp.float32), axis=1))
    residual = (hidden_in.astype(jnp.float32) + proj_sum).astype(jnp.bfloat16)
    wide = residual.astype(jnp.float32)
    mean_square = lax.optimization_barrier(jnp.mean(wide * wide, axis=1))
    normed = (wide * lax.rsqrt(mean_square + 1e-06)[:, None] * norm_gain.astype(jnp.float32)[None, :]).astype(jnp.bfloat16)

    def one_expert(total, inputs):
        expert_gate_up, expert_down, number = inputs
        pre = jnp.dot(normed, expert_gate_up, preferred_element_type=jnp.float32)
        hidden = (jax.nn.silu(pre[:, :FF]) * pre[:, FF:]).astype(jnp.bfloat16)
        result = jnp.dot(hidden, expert_down, preferred_element_type=jnp.float32).astype(jnp.bfloat16)
        row_weight = lax.optimization_barrier(jnp.sum(jnp.where(expert_ids == number, gate_probs, 0.0), axis=1))
        return (total + row_weight[:, None] * result.astype(jnp.float32), None)
    start = jnp.zeros((ROWS, D), jnp.float32)
    mixture, unused = lax.scan(one_expert, start, (gate_up, down_proj, jnp.arange(EXPERTS, dtype=jnp.int32)))
    return (wide + mixture).astype(jnp.bfloat16)
```

```python
import functools
import math

import jax
import jax.numpy as jnp
from jax import lax
from jax.experimental import pallas as pl
from jax.experimental.pallas import tpu as pltpu
from jax.sharding import PartitionSpec as P

HD = 128
KV = 4
MOST = 2


neg_large = -1e30


def body(
    hidden_in,
    queries,
    cache_keys,
    cache_values,
    new_key,
    new_value,
    cache_lengths,
    out_weight,
    norm_gain,
    gate_probs,
    expert_ids,
    gate_up,
    down_proj,
):
    row_count = queries.shape[0]
    head_count = queries.shape[1] // HD
    group_size = head_count // KV
    local_length = cache_keys.shape[1]
    score_scale = 1.0 / math.sqrt(HD)
    tensor_pos = lax.axis_index("tensor")
    tensor_count = lax.axis_size("tensor")
    my_heads = head_count // tensor_count
    query_heads = queries.reshape(row_count, KV, group_size, HD)
    key_heads = cache_keys.reshape(row_count, local_length, KV, HD)
    value_heads = cache_values.reshape(row_count, local_length, KV, HD)
    scores = (
        jnp.einsum("rkgd,rpkd->rkgp", query_heads, key_heads, preferred_element_type=jnp.float32)
        * score_scale
    )
    position = tensor_pos * local_length + jnp.arange(local_length, dtype=jnp.int32)
    live_mask = (position[None, :] < cache_lengths[:, None])[:, None, None, :]
    local_high = jnp.max(jnp.where(live_mask, scores, neg_large), axis=3)
    own_score = (
        jnp.einsum(
            "rkgd,rkd->rkg",
            query_heads,
            new_key.reshape(row_count, KV, HD),
            preferred_element_type=jnp.float32,
        )
        * score_scale
    )
    own_mine = lax.dynamic_slice_in_dim(
        own_score.reshape(row_count, head_count), tensor_pos * my_heads, my_heads, 1
    )
    global_high = lax.pmax(local_high, "tensor")
    highest = jnp.maximum(global_high, own_score)
    weights = jnp.where(live_mask, jnp.exp(scores - highest[..., None]), 0.0)
    weight_totals = jnp.sum(weights, axis=3).reshape(row_count, head_count)
    value_sums = jnp.einsum(
        "rkgp,rpkd->rkgd",
        weights.astype(jnp.bfloat16),
        value_heads,
        preferred_element_type=jnp.float32,
    )
    value_sums = value_sums.reshape(row_count, head_count * HD)
    head_values, head_totals = (
        lax.psum_scatter(
            value_sums.astype(jnp.bfloat16), "tensor", scatter_dimension=1, tiled=True
        ).astype(jnp.float32),
        lax.psum_scatter(
            weight_totals.astype(jnp.bfloat16), "tensor", scatter_dimension=1, tiled=True
        ).astype(jnp.float32),
    )
    highest_mine = lax.dynamic_slice_in_dim(
        highest.reshape(row_count, head_count), tensor_pos * my_heads, my_heads, 1
    )
    own_weight = jnp.exp(own_mine - highest_mine)
    own_values = jnp.broadcast_to(
        new_value.reshape(row_count, KV, 1, HD), (row_count, KV, group_size, HD)
    )
    own_values = own_values.reshape(row_count, head_count * HD)
    own_values = lax.dynamic_slice_in_dim(own_values, tensor_pos * my_heads * HD, my_heads * HD, 1)
    own_values = own_values.reshape(row_count, my_heads, HD).astype(jnp.float32)
    low_own = lax.optimization_barrier(own_weight.astype(jnp.bfloat16)).astype(jnp.float32)
    numerator = head_values.reshape(row_count, my_heads, HD) + low_own[..., None] * own_values
    attended = (numerator / (head_totals + own_weight)[..., None]).astype(jnp.bfloat16)
    attended = attended.reshape(row_count, my_heads * HD)
    proj_term = jnp.dot(attended, out_weight, preferred_element_type=jnp.float32)
    proj_sum = lax.psum_scatter(
        proj_term.astype(jnp.bfloat16), "tensor", scatter_dimension=1, tiled=True
    ).astype(jnp.float32)
    residual = (hidden_in.astype(jnp.float32) + proj_sum).astype(jnp.bfloat16)
    wide = residual.astype(jnp.float32)
    feature_total = residual.shape[1] * tensor_count
    full = lax.all_gather(residual, "tensor", axis=1, tiled=True).astype(jnp.float32)
    mean_square = jnp.sum(full * full, axis=1) / feature_total
    normed = (
        wide * lax.rsqrt(mean_square + 1e-06)[:, None] * norm_gain.astype(jnp.float32)[None, :]
    ).astype(jnp.bfloat16)
    feat_width = normed.shape[1]
    exp_local = gate_up.shape[0]
    hidden_units = down_proj.shape[1]
    owner_count = lax.axis_size("expert")
    top_count = expert_ids.shape[1]
    expert_total = exp_local * owner_count
    slot_total = expert_total * MOST
    flat_ids = expert_ids.reshape(row_count * top_count)
    matches = (flat_ids[:, None] == jnp.arange(expert_total, dtype=jnp.int32)[None, :]).astype(
        jnp.int32
    )
    earlier = jnp.cumsum(matches, axis=0) - matches
    slot_rank = jnp.sum(earlier * matches, axis=1)
    column = flat_ids % exp_local * (owner_count * MOST) + flat_ids // exp_local * MOST + slot_rank
    placing = (column[:, None] == jnp.arange(slot_total, dtype=jnp.int32)[None, :]).astype(
        jnp.bfloat16
    )
    copies = jnp.broadcast_to(normed[:, None, :], (row_count, top_count, feat_width)).reshape(
        row_count * top_count, feat_width
    )
    outgoing = jnp.einsum("pc,pd->cd", placing, copies, preferred_element_type=jnp.float32).astype(
        jnp.bfloat16
    )
    outgoing = outgoing.reshape(exp_local, owner_count, MOST, feat_width)
    arrived = lax.all_to_all(outgoing, "expert", split_axis=1, concat_axis=1, tiled=True)
    slot_count = arrived.shape[2]
    slot_rows = arrived.reshape(exp_local, owner_count * slot_count, feat_width)
    pre_term = jnp.einsum("erd,edf->erf", slot_rows, gate_up, preferred_element_type=jnp.float32)
    summed = lax.psum(pre_term.astype(jnp.bfloat16), "tensor").astype(jnp.float32)
    hidden = (jax.nn.silu(summed[..., :hidden_units]) * summed[..., hidden_units:]).astype(
        jnp.bfloat16
    )
    result = jnp.einsum(
        "erf,efd->erd", hidden, down_proj, preferred_element_type=jnp.float32
    ).astype(jnp.bfloat16)
    result = result.reshape(exp_local, owner_count, slot_count, feat_width)
    returned = lax.all_to_all(result, "expert", split_axis=1, concat_axis=1, tiled=True)
    pair_out = jnp.dot(
        placing, returned.reshape(slot_total, feat_width), preferred_element_type=jnp.float32
    )
    pair_out = pair_out.reshape(row_count, top_count, feat_width)
    mixture = jnp.einsum("rk,rkd->rd", gate_probs, pair_out)
    return (wide + mixture).astype(jnp.bfloat16)


def fused_kernel(
    tensor_count,
    owner_count,
    hidden_ref,
    query_ref,
    new_key_ref,
    new_value_ref,
    length_ref,
    gain_ref,
    prob_ref,
    id_ref,
    key_hbm,
    value_hbm,
    proj_hbm,
    gate_hbm,
    down_hbm,
    out_ref,
    key_buf,
    value_buf,
    proj_buf,
    gate_buf,
    down_buf,
    part_high,
    part_total,
    part_value,
    stat_all,
    value_all,
    term_all,
    info_all,
    rows_all,
    square_all,
    square_sum,
    slot_rows,
    slot_scale,
    pre_mine,
    pre_got,
    hidden_all,
    result_all,
    mix_mine,
    mix_got,
    load_sem,
    gate_sem,
    down_sem,
    send_sem,
    recv_sem,
    pre_send,
    pre_recv,
    hid_send,
    hid_recv,
):
    rows, width = hidden_ref.shape
    kv_count, group_size = query_ref.shape[1], query_ref.shape[2]
    local_length = key_hbm.shape[1]
    units = down_hbm.shape[1]
    experts = gate_hbm.shape[0]
    half = width // 2
    pairs = experts // 2
    per_owner = pairs // tensor_count
    slots = owner_count * MOST
    gate_slots, down_slots = gate_buf.shape[0], down_buf.shape[0]
    score_scale = 1.0 / math.sqrt(HD)
    t_me = lax.axis_index("tensor")
    e_me = lax.axis_index("expert")

    def t_at(d):
        return lax.rem(t_me + d + tensor_count, tensor_count)

    def e_at(d):
        return lax.rem(e_me + d + owner_count, owner_count)

    def gate_pair(i):
        return t_at(1 + lax.rem(i, tensor_count)) * per_owner + i // tensor_count

    def down_pair(i):
        return t_at(lax.rem(i, tensor_count)) * per_owner + i // tensor_count

    def gate_copy(i):
        slot = lax.rem(i, gate_slots)
        return pltpu.make_async_copy(
            gate_hbm.at[pl.ds(gate_pair(i) * 2, 2)], gate_buf.at[slot], gate_sem.at[slot]
        )

    def down_copy(i):
        slot = lax.rem(i, down_slots)
        return pltpu.make_async_copy(
            down_hbm.at[pl.ds(down_pair(i) * 2, 2)], down_buf.at[slot], down_sem.at[slot]
        )

    def remote(axis, d, kind, src, dst):
        peer = t_at(d) if axis == "tensor" else e_at(d)
        return pltpu.make_async_remote_copy(
            src_ref=src,
            dst_ref=dst,
            send_sem=send_sem.at[kind, d - 1],
            recv_sem=recv_sem.at[kind, d - 1],
            device_id={axis: peer},
            device_id_type=pl.DeviceIdType.MESH,
        )

    t_offsets = range(1, tensor_count)
    e_offsets = range(1, owner_count)

    key_copy = pltpu.make_async_copy(key_hbm, key_buf, load_sem.at[0])
    value_copy = pltpu.make_async_copy(value_hbm, value_buf, load_sem.at[1])
    proj_copy = pltpu.make_async_copy(proj_hbm, proj_buf, load_sem.at[2])
    key_copy.start()
    value_copy.start()
    proj_copy.start()

    barrier = pltpu.get_barrier_semaphore()
    for d in t_offsets:
        pl.semaphore_signal(
            barrier, inc=1, device_id={"tensor": t_at(d)}, device_id_type=pl.DeviceIdType.MESH
        )
    for d in e_offsets:
        pl.semaphore_signal(
            barrier, inc=1, device_id={"expert": e_at(d)}, device_id_type=pl.DeviceIdType.MESH
        )

    lane = lax.broadcasted_iota(jnp.int32, (rows, 128), 1)
    row = lax.broadcasted_iota(jnp.int32, (rows, 128), 0)
    named = jnp.zeros((rows, 128), jnp.float32)
    count = jnp.zeros((rows, 128), jnp.float32)
    for k in range(id_ref.shape[1]):
        hit = id_ref[:, k : k + 1] == lane // MOST
        named = named + jnp.where(hit, prob_ref[:, k : k + 1], 0.0)
        count = count + jnp.where(hit, 1.0, 0.0)
    earlier = jnp.zeros((rows, 128), jnp.float32)
    for j in range(rows):
        earlier = earlier + jnp.where(row > j, count[j : j + 1, :], 0.0)
    info_all[e_me] = jnp.where(earlier == (lane % MOST).astype(jnp.float32), named, 0.0)

    key_copy.wait()
    value_copy.wait()
    for i in range(gate_slots):
        gate_copy(i).start()
    for i in range(down_slots):
        down_copy(i).start()

    pl.semaphore_wait(barrier, len(t_offsets) + len(e_offsets))
    info_sends = [remote("expert", d, 0, info_all.at[e_me], info_all.at[e_me]) for d in e_offsets]
    for copy in info_sends:
        copy.start()

    position = t_me * local_length + lax.broadcasted_iota(
        jnp.int32, (kv_count * group_size, local_length), 1
    )
    for r in range(rows):
        live = position < length_ref[r : r + 1, 0:1]
        scores = jnp.concatenate(
            [
                lax.dot_general(
                    query_ref[r, v],
                    key_buf[r, :, v * HD : (v + 1) * HD],
                    (((1,), (1,)), ((), ())),
                    preferred_element_type=jnp.float32,
                )
                for v in range(kv_count)
            ],
            axis=0,
        )
        scores = jnp.where(live, scores * score_scale, neg_large)
        high = jnp.max(scores, axis=1, keepdims=True)
        weights = jnp.where(live, jnp.exp(scores - high), 0.0)
        total = jnp.sum(weights, axis=1, keepdims=True)
        low = weights.astype(jnp.bfloat16)
        for v in range(kv_count):
            span = slice(v * group_size, (v + 1) * group_size)
            at = slice(r * group_size, (r + 1) * group_size)
            part_value[v, at, :] = jnp.dot(
                low[span],
                value_buf[r, :, v * HD : (v + 1) * HD],
                preferred_element_type=jnp.float32,
            )
            part_high[v, at, :] = jnp.broadcast_to(high[span], (group_size, HD))
            part_total[v, at, :] = jnp.broadcast_to(total[span], (group_size, HD))

    heads = rows * group_size
    square = lax.broadcasted_iota(jnp.int32, (heads, 128), 0) == lax.broadcasted_iota(
        jnp.int32, (heads, 128), 1
    )
    for v in range(kv_count):
        value_all[v] = part_value[v].astype(jnp.bfloat16)
        high_row = jnp.sum(jnp.where(square, part_high[v], 0.0), axis=0, keepdims=True)
        total_row = jnp.sum(jnp.where(square, part_total[v], 0.0), axis=0, keepdims=True)
        stat_all[v] = jnp.concatenate(
            [high_row, total_row, jnp.zeros((6, 128), jnp.float32)], axis=0
        )
    part_sends = []
    for d in t_offsets:
        dest = t_at(d)
        part_sends.append(
            remote("tensor", d, 1, value_all.at[dest], value_all.at[kv_count + t_me])
        )
        part_sends.append(remote("tensor", d, 2, stat_all.at[dest], stat_all.at[kv_count + t_me]))
    for copy in part_sends:
        copy.start()

    mine = t_me * HD
    own_key = new_key_ref[:, pl.ds(pl.multiple_of(mine, HD), HD)].astype(jnp.float32)
    own_value = new_value_ref[:, pl.ds(pl.multiple_of(mine, HD), HD)].astype(jnp.float32)

    def spread(block):
        wide_block = jnp.broadcast_to(block[:, None, :], (rows, group_size, HD))
        return wide_block.reshape(heads, HD)

    my_query = query_ref[:, t_me].astype(jnp.float32).reshape(heads, HD)
    own_score = jnp.sum(my_query * spread(own_key), axis=1, keepdims=True) * score_scale
    for copy in part_sends:
        copy.wait_recv()
    highs, totals, values = [], [], []
    for s in range(tensor_count):
        at = jnp.where(s == 0, t_me, kv_count + t_at(-s))
        stats = stat_all[at]
        highs.append(
            jnp.sum(
                jnp.where(square, jnp.broadcast_to(stats[0:1], (heads, 128)), 0.0),
                axis=1,
                keepdims=True,
            )
        )
        totals.append(
            jnp.sum(
                jnp.where(square, jnp.broadcast_to(stats[1:2], (heads, 128)), 0.0),
                axis=1,
                keepdims=True,
            )
        )
        values.append(value_all[at].astype(jnp.float32))
    highest = own_score
    for high in highs:
        highest = jnp.maximum(highest, high)
    own_weight = jnp.exp(own_score - highest)
    total = own_weight
    numerator = own_weight.astype(jnp.bfloat16).astype(jnp.float32) * spread(own_value)
    for high, part, value in zip(highs, totals, values):
        factor = jnp.exp(high - highest)
        total = total + factor * part
        numerator = numerator + factor * value
    attended = (numerator / total).astype(jnp.bfloat16)
    to_row = lax.broadcasted_iota(jnp.int32, (heads, heads), 0)
    from_row = lax.broadcasted_iota(jnp.int32, (heads, heads), 1)
    swap = (from_row == (to_row % rows) * group_size + to_row // rows).astype(jnp.bfloat16)
    by_head = jnp.dot(swap, attended, preferred_element_type=jnp.float32)
    attended = jnp.concatenate(
        [by_head[h * rows : (h + 1) * rows] for h in range(group_size)], axis=1
    ).astype(jnp.bfloat16)

    proj_copy.wait()

    def stack(block):
        return jnp.concatenate([block[:, :half], block[:, half:]], axis=0).astype(jnp.bfloat16)

    def unstack(block):
        block = block.astype(jnp.float32)
        return jnp.concatenate([block[:rows], block[rows:]], axis=1)

    term_sends = []
    for d in list(t_offsets) + [tensor_count]:
        dest = t_at(d % tensor_count)
        term = jnp.dot(
            attended,
            proj_buf[:, pl.ds(pl.multiple_of(dest * width, width), width)],
            preferred_element_type=jnp.float32,
        )
        if d < tensor_count:
            term_all[tensor_count + d] = stack(term)
            copy = remote(
                "tensor", d, 3, term_all.at[tensor_count + d], term_all.at[t_me]
            )
            copy.start()
            term_sends.append(copy)
        else:
            term_all[t_me] = stack(term)
    for copy in term_sends:
        copy.wait_recv()
    proj_sum = unstack(term_all[0])
    for s in range(1, tensor_count):
        proj_sum = proj_sum + unstack(term_all[s])
    residual = (hidden_ref[...].astype(jnp.float32) + proj_sum).astype(jnp.bfloat16)
    wide = residual.astype(jnp.float32)
    rows_all[e_me] = stack(wide * gain_ref[...].astype(jnp.float32))
    square_all[e_me] = jnp.broadcast_to(
        jnp.sum(wide * wide, axis=1, keepdims=True), (rows, 128)
    )
    row_sends = []
    for d in e_offsets:
        row_sends.append(remote("expert", d, 4, rows_all.at[e_me], rows_all.at[e_me]))
        row_sends.append(remote("expert", d, 5, square_all.at[e_me], square_all.at[e_me]))
    for copy in row_sends:
        copy.start()

    for copy in info_sends:
        copy.wait_recv()
    all_rows = owner_count * rows
    slot_total = experts * slots
    info = jnp.concatenate([info_all[b] for b in range(owner_count)], axis=0)

    def picker(shape, slot_dim):
        slot = lax.broadcasted_iota(jnp.int32, shape, slot_dim)
        other = lax.broadcasted_iota(jnp.int32, shape, 1 - slot_dim)
        wanted = e_me * (experts * MOST) + (slot // slots) * MOST + slot % MOST
        return jnp.where(other == wanted, 1.0, 0.0)

    def same_block(shape, slot_dim):
        slot = lax.broadcasted_iota(jnp.int32, shape, slot_dim)
        other = lax.broadcasted_iota(jnp.int32, shape, 1 - slot_dim)
        return (slot // MOST) % owner_count == other // rows

    by_slot = lax.dot_general(
        picker((slot_total, 128), 0),
        info,
        (((1,), (1,)), ((), ())),
        precision=lax.Precision.HIGHEST,
        preferred_element_type=jnp.float32,
    )
    placing = jnp.where(same_block((slot_total, all_rows), 0) & (by_slot > 0.0), 1.0, 0.0)
    by_row = lax.dot_general(
        info,
        picker((slot_total, 128), 0),
        (((1,), (1,)), ((), ())),
        precision=lax.Precision.HIGHEST,
        preferred_element_type=jnp.float32,
    )
    by_row = jnp.where(same_block((all_rows, slot_total), 1), by_row, 0.0)
    gate_high = by_row.astype(jnp.bfloat16)
    gate_low = (by_row - gate_high.astype(jnp.float32)).astype(jnp.bfloat16)

    for copy in row_sends:
        copy.wait_recv()
    gathered = jnp.concatenate([unstack(rows_all[b]) for b in range(owner_count)], axis=0)
    slot_rows[...] = jnp.dot(
        placing.astype(jnp.bfloat16),
        gathered.astype(jnp.bfloat16),
        preferred_element_type=jnp.float32,
    ).astype(jnp.bfloat16)
    square_sum[t_me] = jnp.concatenate([square_all[b] for b in range(owner_count)], axis=0)
    square_sends = [
        remote("tensor", d, 6, square_sum.at[t_me], square_sum.at[t_me]) for d in t_offsets
    ]
    for copy in square_sends:
        copy.start()

    def pre_copy(i):
        d, k = lax.rem(i, tensor_count), i // tensor_count
        return pltpu.make_async_remote_copy(
            src_ref=pre_mine.at[i],
            dst_ref=pre_got.at[k, d],
            send_sem=pre_send.at[k, d],
            recv_sem=pre_recv.at[k, d],
            device_id={"tensor": t_at(1 + d)},
            device_id_type=pl.DeviceIdType.MESH,
        )

    def hid_copy(k, d):
        pair = t_me * per_owner + k
        return pltpu.make_async_remote_copy(
            src_ref=hidden_all.at[pair],
            dst_ref=hidden_all.at[pair],
            send_sem=hid_send.at[k, d - 1],
            recv_sem=hid_recv.at[k, d - 1],
            device_id={"tensor": t_at(d)},
            device_id_type=pl.DeviceIdType.MESH,
        )

    def reduce_pair(k):
        own = k * tensor_count + tensor_count - 1
        total = pre_mine[own].astype(jnp.float32)
        for d in range(tensor_count - 1):
            pre_copy(k * tensor_count + d).wait_recv()
            total = total + pre_got[k, d].astype(jnp.float32)
        pair = t_me * per_owner + k
        scale = slot_scale[pl.ds(pl.multiple_of(pair * 2 * slots, 2 * slots), 2 * slots), 0:1]
        total = total * scale
        gate, up = total[:, :units], total[:, units:]
        hidden_all[pair] = (gate / (1.0 + jnp.exp(-gate)) * up).astype(jnp.bfloat16)
        for d in t_offsets:
            hid_copy(k, d).start()

    lag = 2

    def gate_step(i, carry):
        pair = gate_pair(i)
        slot = lax.rem(i, gate_slots)
        gate_copy(i).wait()
        block = slot_rows[pl.ds(pl.multiple_of(pair * 2 * slots, 2 * slots), 2 * slots), :]
        first = jnp.dot(block, gate_buf[slot, 0], preferred_element_type=jnp.float32)
        second = jnp.dot(block, gate_buf[slot, 1], preferred_element_type=jnp.float32)
        pre_mine[i] = jnp.concatenate([first[:slots], second[slots:]], axis=0).astype(
            jnp.bfloat16
        )

        @pl.when(lax.rem(i, tensor_count) < tensor_count - 1)
        def _():
            pre_copy(i).start()

        @pl.when(i + gate_slots < pairs)
        def _():
            gate_copy(i + gate_slots).start()

        @pl.when(i == 0)
        def _():
            for copy in square_sends:
                copy.wait_recv()
            mean_square = square_sum[0]
            for s in range(1, tensor_count):
                mean_square = mean_square + square_sum[s]
            scale = lax.rsqrt(mean_square / (width * tensor_count) + 1e-06)
            slot_scale[...] = jnp.dot(
                placing,
                scale,
                precision=lax.Precision.HIGHEST,
                preferred_element_type=jnp.float32,
            )

        @pl.when((i - lag >= tensor_count - 1) & (lax.rem(i - lag, tensor_count) == tensor_count - 1))
        def _():
            reduce_pair((i - lag) // tensor_count)

        return carry

    lax.fori_loop(0, pairs, gate_step, 0)
    reduce_pair(per_owner - 1)

    def down_step(i, carry):
        pair = down_pair(i)
        slot = lax.rem(i, down_slots)
        d, k = lax.rem(i, tensor_count), i // tensor_count

        @pl.when(d > 0)
        def _():
            pltpu.make_async_remote_copy(
                src_ref=hidden_all.at[pair],
                dst_ref=hidden_all.at[pair],
                send_sem=hid_send.at[k, tensor_count - d - 1],
                recv_sem=hid_recv.at[k, tensor_count - d - 1],
                device_id={"tensor": t_at(d)},
                device_id_type=pl.DeviceIdType.MESH,
            ).wait_recv()

        down_copy(i).wait()
        block = hidden_all[pair]
        first = jnp.dot(block, down_buf[slot, 0], preferred_element_type=jnp.float32)
        second = jnp.dot(block, down_buf[slot, 1], preferred_element_type=jnp.float32)
        result_all[pl.ds(pl.multiple_of(pair * 2 * slots, 2 * slots), 2 * slots), :] = (
            jnp.concatenate([first[:slots], second[slots:]], axis=0).astype(jnp.bfloat16)
        )

        @pl.when(i + down_slots < pairs)
        def _():
            down_copy(i + down_slots).start()

        return carry

    lax.fori_loop(0, pairs, down_step, 0)

    both = jnp.dot(
        jnp.concatenate([gate_high, gate_low], axis=0),
        result_all[...],
        preferred_element_type=jnp.float32,
    )
    mixture = both[:all_rows] + both[all_rows:]
    for b in range(owner_count):
        mix_mine[b] = mixture[b * rows : (b + 1) * rows]
    mix_sends = [
        remote("expert", d, 7, mix_mine.at[e_at(d)], mix_got.at[d - 1]) for d in e_offsets
    ]
    for copy in mix_sends:
        copy.start()
    for copy in mix_sends:
        copy.wait_recv()
    total = wide + mix_mine[e_me]
    for d in e_offsets:
        total = total + mix_got[d - 1]
    out_ref[...] = total.astype(jnp.bfloat16)

    for copy in info_sends + part_sends + term_sends + row_sends + square_sends + mix_sends:
        copy.wait_send()
    for k in range(per_owner):
        for d in range(tensor_count - 1):
            pre_copy(k * tensor_count + d).wait_send()
            hid_copy(k, d + 1).wait_send()


def fits_kernel(shapes, tensor_count, owner_count):
    queries, keys, gate_up, down_proj = shapes
    rows = queries[0]
    head_count = queries[1] // HD
    experts = gate_up[0]
    return (
        tensor_count == KV
        and rows == 8
        and head_count == 8 * KV
        and owner_count * MOST == 8
        and experts * owner_count * MOST == 128
        and experts % (2 * tensor_count) == 0
        and gate_up[1] % 256 == 0
        and down_proj[1] % 128 == 0
        and keys[1] % 128 == 0
    )


def fused(
    hidden_in,
    queries,
    cache_keys,
    cache_values,
    new_key,
    new_value,
    cache_lengths,
    out_weight,
    norm_gain,
    gate_probs,
    expert_ids,
    gate_up,
    down_proj,
):
    tensor_count = lax.axis_size("tensor")
    owner_count = lax.axis_size("expert")
    rows, width = hidden_in.shape
    group_size = queries.shape[1] // HD // KV
    experts, units = gate_up.shape[0], down_proj.shape[1]
    pairs = experts // 2
    per_owner = pairs // tensor_count
    slots = owner_count * MOST
    heads = rows * group_size
    half = width // 2
    vmem = pl.BlockSpec(memory_space=pltpu.VMEM)
    far = pl.BlockSpec(memory_space=pl.ANY)
    dma = pltpu.SemaphoreType.DMA
    f32, bf16 = jnp.float32, jnp.bfloat16
    gate_slots, down_slots = min(5, pairs), min(4, pairs)
    others = max(tensor_count, owner_count) - 1
    return pl.pallas_call(
        functools.partial(fused_kernel, tensor_count, owner_count),
        out_shape=jax.ShapeDtypeStruct((rows, width), bf16),
        in_specs=[vmem] * 8 + [far] * 5,
        out_specs=vmem,
        scratch_shapes=[
            pltpu.VMEM(cache_keys.shape, bf16),
            pltpu.VMEM(cache_values.shape, bf16),
            pltpu.VMEM(out_weight.shape, bf16),
            pltpu.VMEM((gate_slots, 2) + gate_up.shape[1:], bf16),
            pltpu.VMEM((down_slots, 2) + down_proj.shape[1:], bf16),
            pltpu.VMEM((KV, heads, HD), f32),
            pltpu.VMEM((KV, heads, HD), f32),
            pltpu.VMEM((KV, heads, HD), f32),
            pltpu.VMEM((KV + tensor_count, 8, 128), f32),
            pltpu.VMEM((KV + tensor_count, heads, HD), bf16),
            pltpu.VMEM((2 * tensor_count, 2 * rows, half), bf16),
            pltpu.VMEM((owner_count, rows, 128), f32),
            pltpu.VMEM((owner_count, 2 * rows, half), bf16),
            pltpu.VMEM((owner_count, rows, 128), f32),
            pltpu.VMEM((tensor_count, owner_count * rows, 128), f32),
            pltpu.VMEM((experts * slots, width), bf16),
            pltpu.VMEM((experts * slots, 128), f32),
            pltpu.VMEM((pairs, 2 * slots, 2 * units), bf16),
            pltpu.VMEM((per_owner, tensor_count - 1, 2 * slots, 2 * units), bf16),
            pltpu.VMEM((pairs, 2 * slots, units), bf16),
            pltpu.VMEM((experts * slots, width), bf16),
            pltpu.VMEM((owner_count, rows, width), f32),
            pltpu.VMEM((owner_count - 1, rows, width), f32),
            dma((3,)),
            dma((gate_slots,)),
            dma((down_slots,)),
            dma((8, others)),
            dma((8, others)),
            dma((per_owner, tensor_count - 1)),
            dma((per_owner, tensor_count - 1)),
            dma((per_owner, tensor_count - 1)),
            dma((per_owner, tensor_count - 1)),
        ],
        compiler_params=pltpu.CompilerParams(
            collective_id=0, has_side_effects=True, vmem_limit_bytes=62 * 1024 * 1024
        ),
    )(
        hidden_in,
        queries.reshape(rows, KV, group_size, HD),
        new_key,
        new_value,
        jnp.broadcast_to(cache_lengths[:, None], (rows, 128)),
        norm_gain[None, :],
        gate_probs,
        expert_ids,
        cache_keys,
        cache_values,
        out_weight,
        gate_up,
        down_proj,
    )


def layer(*args):
    shapes = (args[1].shape, args[2].shape, args[11].shape, args[12].shape)
    if fits_kernel(shapes, lax.axis_size("tensor"), lax.axis_size("expert")):
        return fused(*args)
    return body(*args)


def solution(mesh):
    return jax.shard_map(
        layer,
        mesh=mesh,
        in_specs=(
            P(("groups", "expert"), "tensor"),
            P(("groups", "expert"), None),
            P(("groups", "expert"), "tensor", None),
            P(("groups", "expert"), "tensor", None),
            P(("groups", "expert"), None),
            P(("groups", "expert"), None),
            P(("groups", "expert")),
            P("tensor", None),
            P("tensor"),
            P(("groups", "expert"), None),
            P(("groups", "expert"), None),
            P("expert", "tensor", None),
            P("expert", None, "tensor"),
        ),
        out_specs=P(("groups", "expert"), "tensor"),
        check_vma=False,
    )
```

```python
import functools
import math

import jax
import jax.numpy as jnp
from jax import lax
from jax.experimental import pallas as pl
from jax.experimental.pallas import tpu as pltpu
from jax.sharding import PartitionSpec as P

HD = 128
KV = 4
MOST = 2


neg_large = -1e30


def body(
    hidden_in,
    queries,
    cache_keys,
    cache_values,
    new_key,
    new_value,
    cache_lengths,
    out_weight,
    norm_gain,
    gate_probs,
    expert_ids,
    gate_up,
    down_proj,
):
    row_count = queries.shape[0]
    head_count = queries.shape[1] // HD
    group_size = head_count // KV
    local_length = cache_keys.shape[1]
    score_scale = 1.0 / math.sqrt(HD)
    tensor_pos = lax.axis_index("tensor")
    tensor_count = lax.axis_size("tensor")
    my_heads = head_count // tensor_count
    query_heads = queries.reshape(row_count, KV, group_size, HD)
    key_heads = cache_keys.reshape(row_count, local_length, KV, HD)
    value_heads = cache_values.reshape(row_count, local_length, KV, HD)
    scores = (
        jnp.einsum("rkgd,rpkd->rkgp", query_heads, key_heads, preferred_element_type=jnp.float32)
        * score_scale
    )
    position = tensor_pos * local_length + jnp.arange(local_length, dtype=jnp.int32)
    live_mask = (position[None, :] < cache_lengths[:, None])[:, None, None, :]
    local_high = jnp.max(jnp.where(live_mask, scores, neg_large), axis=3)
    own_score = (
        jnp.einsum(
            "rkgd,rkd->rkg",
            query_heads,
            new_key.reshape(row_count, KV, HD),
            preferred_element_type=jnp.float32,
        )
        * score_scale
    )
    own_mine = lax.dynamic_slice_in_dim(
        own_score.reshape(row_count, head_count), tensor_pos * my_heads, my_heads, 1
    )
    global_high = lax.pmax(local_high, "tensor")
    highest = jnp.maximum(global_high, own_score)
    weights = jnp.where(live_mask, jnp.exp(scores - highest[..., None]), 0.0)
    weight_totals = jnp.sum(weights, axis=3).reshape(row_count, head_count)
    value_sums = jnp.einsum(
        "rkgp,rpkd->rkgd",
        weights.astype(jnp.bfloat16),
        value_heads,
        preferred_element_type=jnp.float32,
    )
    value_sums = value_sums.reshape(row_count, head_count * HD)
    head_values, head_totals = (
        lax.psum_scatter(
            value_sums.astype(jnp.bfloat16), "tensor", scatter_dimension=1, tiled=True
        ).astype(jnp.float32),
        lax.psum_scatter(
            weight_totals.astype(jnp.bfloat16), "tensor", scatter_dimension=1, tiled=True
        ).astype(jnp.float32),
    )
    highest_mine = lax.dynamic_slice_in_dim(
        highest.reshape(row_count, head_count), tensor_pos * my_heads, my_heads, 1
    )
    own_weight = jnp.exp(own_mine - highest_mine)
    own_values = jnp.broadcast_to(
        new_value.reshape(row_count, KV, 1, HD), (row_count, KV, group_size, HD)
    )
    own_values = own_values.reshape(row_count, head_count * HD)
    own_values = lax.dynamic_slice_in_dim(own_values, tensor_pos * my_heads * HD, my_heads * HD, 1)
    own_values = own_values.reshape(row_count, my_heads, HD).astype(jnp.float32)
    low_own = lax.optimization_barrier(own_weight.astype(jnp.bfloat16)).astype(jnp.float32)
    numerator = head_values.reshape(row_count, my_heads, HD) + low_own[..., None] * own_values
    attended = (numerator / (head_totals + own_weight)[..., None]).astype(jnp.bfloat16)
    attended = attended.reshape(row_count, my_heads * HD)
    proj_term = jnp.dot(attended, out_weight, preferred_element_type=jnp.float32)
    proj_sum = lax.psum_scatter(
        proj_term.astype(jnp.bfloat16), "tensor", scatter_dimension=1, tiled=True
    ).astype(jnp.float32)
    residual = (hidden_in.astype(jnp.float32) + proj_sum).astype(jnp.bfloat16)
    wide = residual.astype(jnp.float32)
    feature_total = residual.shape[1] * tensor_count
    full = lax.all_gather(residual, "tensor", axis=1, tiled=True).astype(jnp.float32)
    mean_square = jnp.sum(full * full, axis=1) / feature_total
    normed = (
        wide * lax.rsqrt(mean_square + 1e-06)[:, None] * norm_gain.astype(jnp.float32)[None, :]
    ).astype(jnp.bfloat16)
    feat_width = normed.shape[1]
    exp_local = gate_up.shape[0]
    hidden_units = down_proj.shape[1]
    owner_count = lax.axis_size("expert")
    top_count = expert_ids.shape[1]
    expert_total = exp_local * owner_count
    slot_total = expert_total * MOST
    flat_ids = expert_ids.reshape(row_count * top_count)
    matches = (flat_ids[:, None] == jnp.arange(expert_total, dtype=jnp.int32)[None, :]).astype(
        jnp.int32
    )
    earlier = jnp.cumsum(matches, axis=0) - matches
    slot_rank = jnp.sum(earlier * matches, axis=1)
    column = flat_ids % exp_local * (owner_count * MOST) + flat_ids // exp_local * MOST + slot_rank
    placing = (column[:, None] == jnp.arange(slot_total, dtype=jnp.int32)[None, :]).astype(
        jnp.bfloat16
    )
    copies = jnp.broadcast_to(normed[:, None, :], (row_count, top_count, feat_width)).reshape(
        row_count * top_count, feat_width
    )
    outgoing = jnp.einsum("pc,pd->cd", placing, copies, preferred_element_type=jnp.float32).astype(
        jnp.bfloat16
    )
    outgoing = outgoing.reshape(exp_local, owner_count, MOST, feat_width)
    arrived = lax.all_to_all(outgoing, "expert", split_axis=1, concat_axis=1, tiled=True)
    slot_count = arrived.shape[2]
    slot_rows = arrived.reshape(exp_local, owner_count * slot_count, feat_width)
    pre_term = jnp.einsum("erd,edf->erf", slot_rows, gate_up, preferred_element_type=jnp.float32)
    summed = lax.psum(pre_term.astype(jnp.bfloat16), "tensor").astype(jnp.float32)
    hidden = (jax.nn.silu(summed[..., :hidden_units]) * summed[..., hidden_units:]).astype(
        jnp.bfloat16
    )
    result = jnp.einsum(
        "erf,efd->erd", hidden, down_proj, preferred_element_type=jnp.float32
    ).astype(jnp.bfloat16)
    result = result.reshape(exp_local, owner_count, slot_count, feat_width)
    returned = lax.all_to_all(result, "expert", split_axis=1, concat_axis=1, tiled=True)
    pair_out = jnp.dot(
        placing, returned.reshape(slot_total, feat_width), preferred_element_type=jnp.float32
    )
    pair_out = pair_out.reshape(row_count, top_count, feat_width)
    mixture = jnp.einsum("rk,rkd->rd", gate_probs, pair_out)
    return (wide + mixture).astype(jnp.bfloat16)


def fused_kernel(
    tensor_count,
    owner_count,
    hidden_ref,
    query_ref,
    new_key_ref,
    new_value_ref,
    length_ref,
    gain_ref,
    prob_ref,
    id_ref,
    key_hbm,
    value_hbm,
    proj_hbm,
    gate_hbm,
    down_hbm,
    out_ref,
    key_buf,
    value_buf,
    proj_buf,
    gate_buf,
    down_buf,
    query_heads,
    part_high,
    part_total,
    part_value,
    stat_all,
    value_all,
    term_all,
    info_all,
    rows_all,
    square_all,
    square_sum,
    slot_rows,
    slot_scale,
    pre_mine,
    pre_got,
    hidden_all,
    result_all,
    mix_mine,
    mix_got,
    load_sem,
    gate_sem,
    down_sem,
    send_sem,
    recv_sem,
    pre_send,
    pre_recv,
    hid_send,
    hid_recv,
):
    rows, width = hidden_ref.shape
    kv_count = KV
    head_count = query_ref.shape[1] // HD
    group_size = head_count // KV
    local_length = key_hbm.shape[1]
    units = down_hbm.shape[1]
    experts = gate_hbm.shape[0]
    half = width // 2
    pairs = experts // 2
    per_owner = pairs // tensor_count
    slots = owner_count * MOST
    gate_slots, down_slots = gate_buf.shape[0], down_buf.shape[0]
    score_scale = 1.0 / math.sqrt(HD)
    t_me = lax.axis_index("tensor")
    e_me = lax.axis_index("expert")

    def t_at(d):
        return lax.rem(t_me + d + tensor_count, tensor_count)

    def e_at(d):
        return lax.rem(e_me + d + owner_count, owner_count)

    def gate_pair(i):
        return t_at(1 + lax.rem(i, tensor_count)) * per_owner + i // tensor_count

    def down_pair(i):
        return t_at(lax.rem(i, tensor_count)) * per_owner + i // tensor_count

    def gate_copy(i):
        slot = lax.rem(i, gate_slots)
        return pltpu.make_async_copy(
            gate_hbm.at[pl.ds(gate_pair(i) * 2, 2)], gate_buf.at[slot], gate_sem.at[slot]
        )

    def down_copy(i):
        slot = lax.rem(i, down_slots)
        return pltpu.make_async_copy(
            down_hbm.at[pl.ds(down_pair(i) * 2, 2)], down_buf.at[slot], down_sem.at[slot]
        )

    def remote(axis, d, kind, src, dst):
        peer = t_at(d) if axis == "tensor" else e_at(d)
        return pltpu.make_async_remote_copy(
            src_ref=src,
            dst_ref=dst,
            send_sem=send_sem.at[kind, d - 1],
            recv_sem=recv_sem.at[kind, d - 1],
            device_id={axis: peer},
            device_id_type=pl.DeviceIdType.MESH,
        )

    t_offsets = range(1, tensor_count)
    e_offsets = range(1, owner_count)

    key_copy = pltpu.make_async_copy(key_hbm, key_buf, load_sem.at[0])
    value_copy = pltpu.make_async_copy(value_hbm, value_buf, load_sem.at[1])
    proj_copy = pltpu.make_async_copy(proj_hbm, proj_buf, load_sem.at[2])
    key_copy.start()
    value_copy.start()
    proj_copy.start()

    barrier = pltpu.get_barrier_semaphore()
    for d in t_offsets:
        pl.semaphore_signal(
            barrier, inc=1, device_id={"tensor": t_at(d)}, device_id_type=pl.DeviceIdType.MESH
        )
    for d in e_offsets:
        pl.semaphore_signal(
            barrier, inc=1, device_id={"expert": e_at(d)}, device_id_type=pl.DeviceIdType.MESH
        )

    lane = lax.broadcasted_iota(jnp.int32, (rows, 128), 1)
    row = lax.broadcasted_iota(jnp.int32, (rows, 128), 0)
    named = jnp.zeros((rows, 128), jnp.float32)
    count = jnp.zeros((rows, 128), jnp.float32)
    for k in range(id_ref.shape[1]):
        hit = id_ref[:, k : k + 1] == lane // MOST
        named = named + jnp.where(hit, prob_ref[:, k : k + 1], 0.0)
        count = count + jnp.where(hit, 1.0, 0.0)
    earlier = jnp.zeros((rows, 128), jnp.float32)
    for j in range(rows):
        earlier = earlier + jnp.where(row > j, count[j : j + 1, :], 0.0)
    info_all[e_me] = jnp.where(earlier == (lane % MOST).astype(jnp.float32), named, 0.0)

    for h in range(head_count):
        query_heads[h * rows : (h + 1) * rows, :] = query_ref[:, h * HD : (h + 1) * HD].astype(
            jnp.float32
        )

    key_copy.wait()
    value_copy.wait()
    for i in range(gate_slots):
        gate_copy(i).start()
    for i in range(down_slots):
        down_copy(i).start()

    pl.semaphore_wait(barrier, len(t_offsets) + len(e_offsets))
    info_sends = [remote("expert", d, 0, info_all.at[e_me], info_all.at[e_me]) for d in e_offsets]
    for copy in info_sends:
        copy.start()

    position = t_me * local_length + lax.broadcasted_iota(
        jnp.int32, (kv_count * group_size, local_length), 1
    )
    for r in range(rows):
        live = position < length_ref[r]
        query = query_heads[pl.ds(r, head_count, stride=rows), :].astype(jnp.bfloat16)
        scores = jnp.concatenate(
            [
                lax.dot_general(
                    query[v * group_size : (v + 1) * group_size],
                    key_buf[r, :, v * HD : (v + 1) * HD],
                    (((1,), (1,)), ((), ())),
                    preferred_element_type=jnp.float32,
                )
                for v in range(kv_count)
            ],
            axis=0,
        )
        scores = jnp.where(live, scores * score_scale, neg_large)
        high = jnp.max(scores, axis=1, keepdims=True)
        weights = jnp.where(live, jnp.exp(scores - high), 0.0)
        total = jnp.sum(weights, axis=1, keepdims=True)
        low = weights.astype(jnp.bfloat16)
        for v in range(kv_count):
            span = slice(v * group_size, (v + 1) * group_size)
            at = slice(r * group_size, (r + 1) * group_size)
            part_value[v, at, :] = jnp.dot(
                low[span],
                value_buf[r, :, v * HD : (v + 1) * HD],
                preferred_element_type=jnp.float32,
            )
            part_high[v, at, :] = jnp.broadcast_to(high[span], (group_size, HD))
            part_total[v, at, :] = jnp.broadcast_to(total[span], (group_size, HD))

    heads = rows * group_size
    square = lax.broadcasted_iota(jnp.int32, (heads, 128), 0) == lax.broadcasted_iota(
        jnp.int32, (heads, 128), 1
    )
    for v in range(kv_count):
        value_all[v] = part_value[v].astype(jnp.bfloat16)
        high_row = jnp.sum(jnp.where(square, part_high[v], 0.0), axis=0, keepdims=True)
        total_row = jnp.sum(jnp.where(square, part_total[v], 0.0), axis=0, keepdims=True)
        stat_all[v] = jnp.concatenate(
            [high_row, total_row, jnp.zeros((6, 128), jnp.float32)], axis=0
        )
    part_sends = []
    for d in t_offsets:
        dest = t_at(d)
        part_sends.append(
            remote("tensor", d, 1, value_all.at[dest], value_all.at[kv_count + t_me])
        )
        part_sends.append(remote("tensor", d, 2, stat_all.at[dest], stat_all.at[kv_count + t_me]))
    for copy in part_sends:
        copy.start()

    mine = t_me * HD
    own_key = new_key_ref[:, pl.ds(pl.multiple_of(mine, HD), HD)].astype(jnp.float32)
    own_value = new_value_ref[:, pl.ds(pl.multiple_of(mine, HD), HD)].astype(jnp.float32)

    def spread(block):
        wide_block = jnp.broadcast_to(block[:, None, :], (rows, group_size, HD))
        return wide_block.reshape(heads, HD)

    my_query = jnp.concatenate(
        [
            query_heads[pl.ds(t_me * heads + r, group_size, stride=rows), :]
            for r in range(rows)
        ],
        axis=0,
    )
    own_score = jnp.sum(my_query * spread(own_key), axis=1, keepdims=True) * score_scale
    for copy in part_sends:
        copy.wait_recv()
    highs, totals, values = [], [], []
    for s in range(tensor_count):
        at = jnp.where(s == 0, t_me, kv_count + t_at(-s))
        stats = stat_all[at]
        highs.append(
            jnp.sum(
                jnp.where(square, jnp.broadcast_to(stats[0:1], (heads, 128)), 0.0),
                axis=1,
                keepdims=True,
            )
        )
        totals.append(
            jnp.sum(
                jnp.where(square, jnp.broadcast_to(stats[1:2], (heads, 128)), 0.0),
                axis=1,
                keepdims=True,
            )
        )
        values.append(value_all[at].astype(jnp.float32))
    highest = own_score
    for high in highs:
        highest = jnp.maximum(highest, high)
    own_weight = jnp.exp(own_score - highest)
    total = own_weight
    numerator = own_weight.astype(jnp.bfloat16).astype(jnp.float32) * spread(own_value)
    for high, part, value in zip(highs, totals, values):
        factor = jnp.exp(high - highest)
        total = total + factor * part
        numerator = numerator + factor * value
    attended = (numerator / total).astype(jnp.bfloat16)
    to_row = lax.broadcasted_iota(jnp.int32, (heads, heads), 0)
    from_row = lax.broadcasted_iota(jnp.int32, (heads, heads), 1)
    swap = (from_row == (to_row % rows) * group_size + to_row // rows).astype(jnp.bfloat16)
    by_head = jnp.dot(swap, attended, preferred_element_type=jnp.float32)
    attended = jnp.concatenate(
        [by_head[h * rows : (h + 1) * rows] for h in range(group_size)], axis=1
    ).astype(jnp.bfloat16)

    proj_copy.wait()

    def stack(block):
        return jnp.concatenate([block[:, :half], block[:, half:]], axis=0).astype(jnp.bfloat16)

    def unstack(block):
        block = block.astype(jnp.float32)
        return jnp.concatenate([block[:rows], block[rows:]], axis=1)

    term_sends = []
    for d in list(t_offsets) + [tensor_count]:
        dest = t_at(d % tensor_count)
        term = jnp.dot(
            attended,
            proj_buf[:, pl.ds(pl.multiple_of(dest * width, width), width)],
            preferred_element_type=jnp.float32,
        )
        if d < tensor_count:
            term_all[tensor_count + d] = stack(term)
            copy = remote(
                "tensor", d, 3, term_all.at[tensor_count + d], term_all.at[t_me]
            )
            copy.start()
            term_sends.append(copy)
        else:
            term_all[t_me] = stack(term)
    for copy in term_sends:
        copy.wait_recv()
    proj_sum = unstack(term_all[0])
    for s in range(1, tensor_count):
        proj_sum = proj_sum + unstack(term_all[s])
    residual = (hidden_ref[...].astype(jnp.float32) + proj_sum).astype(jnp.bfloat16)
    wide = residual.astype(jnp.float32)
    rows_all[e_me] = stack(wide * gain_ref[...].astype(jnp.float32).reshape(1, width))
    square_all[e_me] = jnp.broadcast_to(
        jnp.sum(wide * wide, axis=1, keepdims=True), (rows, 128)
    )
    row_sends = []
    for d in e_offsets:
        row_sends.append(remote("expert", d, 4, rows_all.at[e_me], rows_all.at[e_me]))
        row_sends.append(remote("expert", d, 5, square_all.at[e_me], square_all.at[e_me]))
    for copy in row_sends:
        copy.start()

    for copy in info_sends:
        copy.wait_recv()
    all_rows = owner_count * rows
    slot_total = experts * slots
    info = jnp.concatenate([info_all[b] for b in range(owner_count)], axis=0)

    def picker(shape, slot_dim):
        slot = lax.broadcasted_iota(jnp.int32, shape, slot_dim)
        other = lax.broadcasted_iota(jnp.int32, shape, 1 - slot_dim)
        wanted = e_me * (experts * MOST) + (slot // slots) * MOST + slot % MOST
        return jnp.where(other == wanted, 1.0, 0.0)

    def same_block(shape, slot_dim):
        slot = lax.broadcasted_iota(jnp.int32, shape, slot_dim)
        other = lax.broadcasted_iota(jnp.int32, shape, 1 - slot_dim)
        return (slot // MOST) % owner_count == other // rows

    by_slot = lax.dot_general(
        picker((slot_total, 128), 0),
        info,
        (((1,), (1,)), ((), ())),
        precision=lax.Precision.HIGHEST,
        preferred_element_type=jnp.float32,
    )
    placing = jnp.where(same_block((slot_total, all_rows), 0) & (by_slot > 0.0), 1.0, 0.0)
    by_row = lax.dot_general(
        info,
        picker((slot_total, 128), 0),
        (((1,), (1,)), ((), ())),
        precision=lax.Precision.HIGHEST,
        preferred_element_type=jnp.float32,
    )
    by_row = jnp.where(same_block((all_rows, slot_total), 1), by_row, 0.0)
    gate_high = by_row.astype(jnp.bfloat16)
    gate_low = (by_row - gate_high.astype(jnp.float32)).astype(jnp.bfloat16)

    for copy in row_sends:
        copy.wait_recv()
    gathered = jnp.concatenate([unstack(rows_all[b]) for b in range(owner_count)], axis=0)
    slot_rows[...] = jnp.dot(
        placing.astype(jnp.bfloat16),
        gathered.astype(jnp.bfloat16),
        preferred_element_type=jnp.float32,
    ).astype(jnp.bfloat16)
    square_sum[t_me] = jnp.concatenate([square_all[b] for b in range(owner_count)], axis=0)
    square_sends = [
        remote("tensor", d, 6, square_sum.at[t_me], square_sum.at[t_me]) for d in t_offsets
    ]
    for copy in square_sends:
        copy.start()

    def pre_copy(i):
        d, k = lax.rem(i, tensor_count), i // tensor_count
        return pltpu.make_async_remote_copy(
            src_ref=pre_mine.at[i],
            dst_ref=pre_got.at[k, d],
            send_sem=pre_send.at[k, d],
            recv_sem=pre_recv.at[k, d],
            device_id={"tensor": t_at(1 + d)},
            device_id_type=pl.DeviceIdType.MESH,
        )

    def hid_copy(k, d):
        pair = t_me * per_owner + k
        return pltpu.make_async_remote_copy(
            src_ref=hidden_all.at[pair],
            dst_ref=hidden_all.at[pair],
            send_sem=hid_send.at[k, d - 1],
            recv_sem=hid_recv.at[k, d - 1],
            device_id={"tensor": t_at(d)},
            device_id_type=pl.DeviceIdType.MESH,
        )

    def reduce_pair(k):
        own = k * tensor_count + tensor_count - 1
        total = pre_mine[own].astype(jnp.float32)
        for d in range(tensor_count - 1):
            pre_copy(k * tensor_count + d).wait_recv()
            total = total + pre_got[k, d].astype(jnp.float32)
        pair = t_me * per_owner + k
        scale = slot_scale[pl.ds(pl.multiple_of(pair * 2 * slots, 2 * slots), 2 * slots), 0:1]
        total = total * scale
        gate, up = total[:, :units], total[:, units:]
        hidden_all[pair] = (gate / (1.0 + jnp.exp(-gate)) * up).astype(jnp.bfloat16)
        for d in t_offsets:
            hid_copy(k, d).start()

    lag = 2

    def gate_step(i, carry):
        pair = gate_pair(i)
        slot = lax.rem(i, gate_slots)
        gate_copy(i).wait()
        block = slot_rows[pl.ds(pl.multiple_of(pair * 2 * slots, 2 * slots), 2 * slots), :]
        first = jnp.dot(block, gate_buf[slot, 0], preferred_element_type=jnp.float32)
        second = jnp.dot(block, gate_buf[slot, 1], preferred_element_type=jnp.float32)
        pre_mine[i] = jnp.concatenate([first[:slots], second[slots:]], axis=0).astype(
            jnp.bfloat16
        )

        @pl.when(lax.rem(i, tensor_count) < tensor_count - 1)
        def _():
            pre_copy(i).start()

        @pl.when(i + gate_slots < pairs)
        def _():
            gate_copy(i + gate_slots).start()

        @pl.when(i == 0)
        def _():
            for copy in square_sends:
                copy.wait_recv()
            mean_square = square_sum[0]
            for s in range(1, tensor_count):
                mean_square = mean_square + square_sum[s]
            scale = lax.rsqrt(mean_square / (width * tensor_count) + 1e-06)
            slot_scale[...] = jnp.dot(
                placing,
                scale,
                precision=lax.Precision.HIGHEST,
                preferred_element_type=jnp.float32,
            )

        @pl.when((i - lag >= tensor_count - 1) & (lax.rem(i - lag, tensor_count) == tensor_count - 1))
        def _():
            reduce_pair((i - lag) // tensor_count)

        return carry

    lax.fori_loop(0, pairs, gate_step, 0)
    reduce_pair(per_owner - 1)

    def down_step(i, carry):
        pair = down_pair(i)
        slot = lax.rem(i, down_slots)
        d, k = lax.rem(i, tensor_count), i // tensor_count

        @pl.when(d > 0)
        def _():
            pltpu.make_async_remote_copy(
                src_ref=hidden_all.at[pair],
                dst_ref=hidden_all.at[pair],
                send_sem=hid_send.at[k, tensor_count - d - 1],
                recv_sem=hid_recv.at[k, tensor_count - d - 1],
                device_id={"tensor": t_at(d)},
                device_id_type=pl.DeviceIdType.MESH,
            ).wait_recv()

        down_copy(i).wait()
        block = hidden_all[pair]
        first = jnp.dot(block, down_buf[slot, 0], preferred_element_type=jnp.float32)
        second = jnp.dot(block, down_buf[slot, 1], preferred_element_type=jnp.float32)
        result_all[pl.ds(pl.multiple_of(pair * 2 * slots, 2 * slots), 2 * slots), :] = (
            jnp.concatenate([first[:slots], second[slots:]], axis=0).astype(jnp.bfloat16)
        )

        @pl.when(i + down_slots < pairs)
        def _():
            down_copy(i + down_slots).start()

        return carry

    lax.fori_loop(0, pairs, down_step, 0)

    both = jnp.dot(
        jnp.concatenate([gate_high, gate_low], axis=0),
        result_all[...],
        preferred_element_type=jnp.float32,
    )
    mixture = both[:all_rows] + both[all_rows:]
    for b in range(owner_count):
        mix_mine[b] = mixture[b * rows : (b + 1) * rows]
    mix_sends = [
        remote("expert", d, 7, mix_mine.at[e_at(d)], mix_got.at[d - 1]) for d in e_offsets
    ]
    for copy in mix_sends:
        copy.start()
    for copy in mix_sends:
        copy.wait_recv()
    total = wide + mix_mine[e_me]
    for d in e_offsets:
        total = total + mix_got[d - 1]
    out_ref[...] = total.astype(jnp.bfloat16)

    for copy in info_sends + part_sends + term_sends + row_sends + square_sends + mix_sends:
        copy.wait_send()
    for k in range(per_owner):
        for d in range(tensor_count - 1):
            pre_copy(k * tensor_count + d).wait_send()
            hid_copy(k, d + 1).wait_send()


def fits_kernel(shapes, tensor_count, owner_count):
    queries, keys, gate_up, down_proj = shapes
    rows = queries[0]
    head_count = queries[1] // HD
    experts = gate_up[0]
    return (
        tensor_count == KV
        and rows == 8
        and head_count == 8 * KV
        and owner_count * MOST == 8
        and experts * owner_count * MOST == 128
        and experts % (2 * tensor_count) == 0
        and gate_up[1] % 256 == 0
        and down_proj[1] % 128 == 0
        and keys[1] % 128 == 0
    )


def fused(
    hidden_in,
    queries,
    cache_keys,
    cache_values,
    new_key,
    new_value,
    cache_lengths,
    out_weight,
    norm_gain,
    gate_probs,
    expert_ids,
    gate_up,
    down_proj,
):
    tensor_count = lax.axis_size("tensor")
    owner_count = lax.axis_size("expert")
    rows, width = hidden_in.shape
    group_size = queries.shape[1] // HD // KV
    experts, units = gate_up.shape[0], down_proj.shape[1]
    pairs = experts // 2
    per_owner = pairs // tensor_count
    slots = owner_count * MOST
    heads = rows * group_size
    half = width // 2
    vmem = pl.BlockSpec(memory_space=pltpu.VMEM)
    far = pl.BlockSpec(memory_space=pl.ANY)
    dma = pltpu.SemaphoreType.DMA
    f32, bf16 = jnp.float32, jnp.bfloat16
    gate_slots, down_slots = min(5, pairs), min(4, pairs)
    others = max(tensor_count, owner_count) - 1
    return pl.pallas_call(
        functools.partial(fused_kernel, tensor_count, owner_count),
        out_shape=jax.ShapeDtypeStruct((rows, width), bf16),
        in_specs=[vmem] * 4
        + [pl.BlockSpec(memory_space=pltpu.SMEM)]
        + [vmem] * 3
        + [far] * 5,
        out_specs=vmem,
        scratch_shapes=[
            pltpu.VMEM(cache_keys.shape, bf16),
            pltpu.VMEM(cache_values.shape, bf16),
            pltpu.VMEM(out_weight.shape, bf16),
            pltpu.VMEM((gate_slots, 2) + gate_up.shape[1:], bf16),
            pltpu.VMEM((down_slots, 2) + down_proj.shape[1:], bf16),
            pltpu.VMEM((KV * heads, HD), f32),
            pltpu.VMEM((KV, heads, HD), f32),
            pltpu.VMEM((KV, heads, HD), f32),
            pltpu.VMEM((KV, heads, HD), f32),
            pltpu.VMEM((KV + tensor_count, 8, 128), f32),
            pltpu.VMEM((KV + tensor_count, heads, HD), bf16),
            pltpu.VMEM((2 * tensor_count, 2 * rows, half), bf16),
            pltpu.VMEM((owner_count, rows, 128), f32),
            pltpu.VMEM((owner_count, 2 * rows, half), bf16),
            pltpu.VMEM((owner_count, rows, 128), f32),
            pltpu.VMEM((tensor_count, owner_count * rows, 128), f32),
            pltpu.VMEM((experts * slots, width), bf16),
            pltpu.VMEM((experts * slots, 128), f32),
            pltpu.VMEM((pairs, 2 * slots, 2 * units), bf16),
            pltpu.VMEM((per_owner, tensor_count - 1, 2 * slots, 2 * units), bf16),
            pltpu.VMEM((pairs, 2 * slots, units), bf16),
            pltpu.VMEM((experts * slots, width), bf16),
            pltpu.VMEM((owner_count, rows, width), f32),
            pltpu.VMEM((owner_count - 1, rows, width), f32),
            dma((3,)),
            dma((gate_slots,)),
            dma((down_slots,)),
            dma((8, others)),
            dma((8, others)),
            dma((per_owner, tensor_count - 1)),
            dma((per_owner, tensor_count - 1)),
            dma((per_owner, tensor_count - 1)),
            dma((per_owner, tensor_count - 1)),
        ],
        compiler_params=pltpu.CompilerParams(
            collective_id=0, has_side_effects=True, vmem_limit_bytes=62 * 1024 * 1024
        ),
    )(
        hidden_in,
        queries,
        new_key,
        new_value,
        cache_lengths,
        norm_gain,
        gate_probs,
        expert_ids,
        cache_keys,
        cache_values,
        out_weight,
        gate_up,
        down_proj,
    )


def layer(*args):
    shapes = (args[1].shape, args[2].shape, args[11].shape, args[12].shape)
    if fits_kernel(shapes, lax.axis_size("tensor"), lax.axis_size("expert")):
        return fused(*args)
    return body(*args)


def solution(mesh):
    return jax.shard_map(
        layer,
        mesh=mesh,
        in_specs=(
            P(("groups", "expert"), "tensor"),
            P(("groups", "expert"), None),
            P(("groups", "expert"), "tensor", None),
            P(("groups", "expert"), "tensor", None),
            P(("groups", "expert"), None),
            P(("groups", "expert"), None),
            P(("groups", "expert")),
            P("tensor", None),
            P("tensor"),
            P(("groups", "expert"), None),
            P(("groups", "expert"), None),
            P("expert", "tensor", None),
            P("expert", None, "tensor"),
        ),
        out_specs=P(("groups", "expert"), "tensor"),
        check_vma=False,
    )
```

```python
import functools
import math

import jax
import jax.numpy as jnp
from jax import lax
from jax.experimental import pallas as pl
from jax.experimental.pallas import tpu as pltpu
from jax.sharding import PartitionSpec as P

HD = 128
KV = 4
MOST = 2


neg_large = -1e30


def body(
    hidden_in,
    queries,
    cache_keys,
    cache_values,
    new_key,
    new_value,
    cache_lengths,
    out_weight,
    norm_gain,
    gate_probs,
    expert_ids,
    gate_up,
    down_proj,
):
    row_count = queries.shape[0]
    head_count = queries.shape[1] // HD
    group_size = head_count // KV
    local_length = cache_keys.shape[1]
    score_scale = 1.0 / math.sqrt(HD)
    tensor_pos = lax.axis_index("tensor")
    tensor_count = lax.axis_size("tensor")
    my_heads = head_count // tensor_count
    query_heads = queries.reshape(row_count, KV, group_size, HD)
    key_heads = cache_keys.reshape(row_count, local_length, KV, HD)
    value_heads = cache_values.reshape(row_count, local_length, KV, HD)
    scores = (
        jnp.einsum("rkgd,rpkd->rkgp", query_heads, key_heads, preferred_element_type=jnp.float32)
        * score_scale
    )
    position = tensor_pos * local_length + jnp.arange(local_length, dtype=jnp.int32)
    live_mask = (position[None, :] < cache_lengths[:, None])[:, None, None, :]
    local_high = jnp.max(jnp.where(live_mask, scores, neg_large), axis=3)
    own_score = (
        jnp.einsum(
            "rkgd,rkd->rkg",
            query_heads,
            new_key.reshape(row_count, KV, HD),
            preferred_element_type=jnp.float32,
        )
        * score_scale
    )
    own_mine = lax.dynamic_slice_in_dim(
        own_score.reshape(row_count, head_count), tensor_pos * my_heads, my_heads, 1
    )
    global_high = lax.pmax(local_high, "tensor")
    highest = jnp.maximum(global_high, own_score)
    weights = jnp.where(live_mask, jnp.exp(scores - highest[..., None]), 0.0)
    weight_totals = jnp.sum(weights, axis=3).reshape(row_count, head_count)
    value_sums = jnp.einsum(
        "rkgp,rpkd->rkgd",
        weights.astype(jnp.bfloat16),
        value_heads,
        preferred_element_type=jnp.float32,
    )
    value_sums = value_sums.reshape(row_count, head_count * HD)
    head_values, head_totals = (
        lax.psum_scatter(
            value_sums.astype(jnp.bfloat16), "tensor", scatter_dimension=1, tiled=True
        ).astype(jnp.float32),
        lax.psum_scatter(
            weight_totals.astype(jnp.bfloat16), "tensor", scatter_dimension=1, tiled=True
        ).astype(jnp.float32),
    )
    highest_mine = lax.dynamic_slice_in_dim(
        highest.reshape(row_count, head_count), tensor_pos * my_heads, my_heads, 1
    )
    own_weight = jnp.exp(own_mine - highest_mine)
    own_values = jnp.broadcast_to(
        new_value.reshape(row_count, KV, 1, HD), (row_count, KV, group_size, HD)
    )
    own_values = own_values.reshape(row_count, head_count * HD)
    own_values = lax.dynamic_slice_in_dim(own_values, tensor_pos * my_heads * HD, my_heads * HD, 1)
    own_values = own_values.reshape(row_count, my_heads, HD).astype(jnp.float32)
    low_own = lax.optimization_barrier(own_weight.astype(jnp.bfloat16)).astype(jnp.float32)
    numerator = head_values.reshape(row_count, my_heads, HD) + low_own[..., None] * own_values
    attended = (numerator / (head_totals + own_weight)[..., None]).astype(jnp.bfloat16)
    attended = attended.reshape(row_count, my_heads * HD)
    proj_term = jnp.dot(attended, out_weight, preferred_element_type=jnp.float32)
    proj_sum = lax.psum_scatter(
        proj_term.astype(jnp.bfloat16), "tensor", scatter_dimension=1, tiled=True
    ).astype(jnp.float32)
    residual = (hidden_in.astype(jnp.float32) + proj_sum).astype(jnp.bfloat16)
    wide = residual.astype(jnp.float32)
    feature_total = residual.shape[1] * tensor_count
    full = lax.all_gather(residual, "tensor", axis=1, tiled=True).astype(jnp.float32)
    mean_square = jnp.sum(full * full, axis=1) / feature_total
    normed = (
        wide * lax.rsqrt(mean_square + 1e-06)[:, None] * norm_gain.astype(jnp.float32)[None, :]
    ).astype(jnp.bfloat16)
    feat_width = normed.shape[1]
    exp_local = gate_up.shape[0]
    hidden_units = down_proj.shape[1]
    owner_count = lax.axis_size("expert")
    top_count = expert_ids.shape[1]
    expert_total = exp_local * owner_count
    slot_total = expert_total * MOST
    flat_ids = expert_ids.reshape(row_count * top_count)
    matches = (flat_ids[:, None] == jnp.arange(expert_total, dtype=jnp.int32)[None, :]).astype(
        jnp.int32
    )
    earlier = jnp.cumsum(matches, axis=0) - matches
    slot_rank = jnp.sum(earlier * matches, axis=1)
    column = flat_ids % exp_local * (owner_count * MOST) + flat_ids // exp_local * MOST + slot_rank
    placing = (column[:, None] == jnp.arange(slot_total, dtype=jnp.int32)[None, :]).astype(
        jnp.bfloat16
    )
    copies = jnp.broadcast_to(normed[:, None, :], (row_count, top_count, feat_width)).reshape(
        row_count * top_count, feat_width
    )
    outgoing = jnp.einsum("pc,pd->cd", placing, copies, preferred_element_type=jnp.float32).astype(
        jnp.bfloat16
    )
    outgoing = outgoing.reshape(exp_local, owner_count, MOST, feat_width)
    arrived = lax.all_to_all(outgoing, "expert", split_axis=1, concat_axis=1, tiled=True)
    slot_count = arrived.shape[2]
    slot_rows = arrived.reshape(exp_local, owner_count * slot_count, feat_width)
    pre_term = jnp.einsum("erd,edf->erf", slot_rows, gate_up, preferred_element_type=jnp.float32)
    summed = lax.psum(pre_term.astype(jnp.bfloat16), "tensor").astype(jnp.float32)
    hidden = (jax.nn.silu(summed[..., :hidden_units]) * summed[..., hidden_units:]).astype(
        jnp.bfloat16
    )
    result = jnp.einsum(
        "erf,efd->erd", hidden, down_proj, preferred_element_type=jnp.float32
    ).astype(jnp.bfloat16)
    result = result.reshape(exp_local, owner_count, slot_count, feat_width)
    returned = lax.all_to_all(result, "expert", split_axis=1, concat_axis=1, tiled=True)
    pair_out = jnp.dot(
        placing, returned.reshape(slot_total, feat_width), preferred_element_type=jnp.float32
    )
    pair_out = pair_out.reshape(row_count, top_count, feat_width)
    mixture = jnp.einsum("rk,rkd->rd", gate_probs, pair_out)
    return (wide + mixture).astype(jnp.bfloat16)


def fused_kernel(
    tensor_count,
    owner_count,
    hidden_ref,
    query_ref,
    new_key_ref,
    new_value_ref,
    length_ref,
    gain_ref,
    prob_ref,
    id_ref,
    key_hbm,
    value_hbm,
    proj_hbm,
    gate_hbm,
    down_hbm,
    out_ref,
    key_buf,
    value_buf,
    proj_buf,
    gate_buf,
    down_buf,
    query_heads,
    part_high,
    part_total,
    part_value,
    stat_all,
    value_all,
    term_all,
    info_all,
    rows_all,
    square_all,
    square_sum,
    slot_rows,
    slot_scale,
    pre_mine,
    pre_got,
    hidden_all,
    result_all,
    mix_mine,
    mix_got,
    load_sem,
    gate_sem,
    down_sem,
    send_sem,
    recv_sem,
    pre_send,
    pre_recv,
    hid_send,
    hid_recv,
):
    rows, width = hidden_ref.shape
    kv_count = KV
    head_count = query_ref.shape[1] // HD
    group_size = head_count // KV
    local_length = key_hbm.shape[1]
    units = down_hbm.shape[1]
    experts = gate_hbm.shape[0]
    half = width // 2
    pairs = experts // 2
    per_owner = pairs // tensor_count
    slots = owner_count * MOST
    gate_slots, down_slots = gate_buf.shape[0], down_buf.shape[0]
    score_scale = 1.0 / math.sqrt(HD)
    t_me = lax.axis_index("tensor")
    e_me = lax.axis_index("expert")

    def t_at(d):
        return lax.rem(t_me + d + tensor_count, tensor_count)

    def e_at(d):
        return lax.rem(e_me + d + owner_count, owner_count)

    def gate_pair(i):
        return t_at(1 + lax.rem(i, tensor_count)) * per_owner + i // tensor_count

    def down_pair(i):
        return t_at(lax.rem(i, tensor_count)) * per_owner + i // tensor_count

    def gate_copy(i):
        slot = lax.rem(i, gate_slots)
        return pltpu.make_async_copy(
            gate_hbm.at[pl.ds(gate_pair(i) * 2, 2)], gate_buf.at[slot], gate_sem.at[slot]
        )

    def down_copy(i):
        slot = lax.rem(i, down_slots)
        return pltpu.make_async_copy(
            down_hbm.at[pl.ds(down_pair(i) * 2, 2)], down_buf.at[slot], down_sem.at[slot]
        )

    def remote(axis, d, kind, src, dst):
        peer = t_at(d) if axis == "tensor" else e_at(d)
        return pltpu.make_async_remote_copy(
            src_ref=src,
            dst_ref=dst,
            send_sem=send_sem.at[kind, d - 1],
            recv_sem=recv_sem.at[kind, d - 1],
            device_id={axis: peer},
            device_id_type=pl.DeviceIdType.MESH,
        )

    t_offsets = range(1, tensor_count)
    e_offsets = range(1, owner_count)

    key_copy = pltpu.make_async_copy(key_hbm, key_buf, load_sem.at[0])
    value_copy = pltpu.make_async_copy(value_hbm, value_buf, load_sem.at[1])
    proj_copy = pltpu.make_async_copy(proj_hbm, proj_buf, load_sem.at[2])
    key_copy.start()
    value_copy.start()

    barrier = pltpu.get_barrier_semaphore()
    for d in t_offsets:
        pl.semaphore_signal(
            barrier, inc=1, device_id={"tensor": t_at(d)}, device_id_type=pl.DeviceIdType.MESH
        )
    for d in e_offsets:
        pl.semaphore_signal(
            barrier, inc=1, device_id={"expert": e_at(d)}, device_id_type=pl.DeviceIdType.MESH
        )

    lane = lax.broadcasted_iota(jnp.int32, (rows, 128), 1)
    row = lax.broadcasted_iota(jnp.int32, (rows, 128), 0)
    named = jnp.zeros((rows, 128), jnp.float32)
    count = jnp.zeros((rows, 128), jnp.float32)
    for k in range(id_ref.shape[1]):
        hit = id_ref[:, k : k + 1] == lane // MOST
        named = named + jnp.where(hit, prob_ref[:, k : k + 1], 0.0)
        count = count + jnp.where(hit, 1.0, 0.0)
    earlier = jnp.zeros((rows, 128), jnp.float32)
    for j in range(rows):
        earlier = earlier + jnp.where(row > j, count[j : j + 1, :], 0.0)
    info_all[e_me] = jnp.where(earlier == (lane % MOST).astype(jnp.float32), named, 0.0)

    for h in range(head_count):
        query_heads[h * rows : (h + 1) * rows, :] = query_ref[:, h * HD : (h + 1) * HD].astype(
            jnp.float32
        )

    key_copy.wait()
    value_copy.wait()
    proj_copy.start()
    for i in range(gate_slots):
        gate_copy(i).start()
    for i in range(down_slots):
        down_copy(i).start()

    pl.semaphore_wait(barrier, len(t_offsets) + len(e_offsets))
    info_sends = [remote("expert", d, 0, info_all.at[e_me], info_all.at[e_me]) for d in e_offsets]
    for copy in info_sends:
        copy.start()

    position = t_me * local_length + lax.broadcasted_iota(
        jnp.int32, (kv_count * group_size, local_length), 1
    )
    for r in range(rows):
        live = position < length_ref[r]
        query = query_heads[pl.ds(r, head_count, stride=rows), :].astype(jnp.bfloat16)
        scores = jnp.concatenate(
            [
                lax.dot_general(
                    query[v * group_size : (v + 1) * group_size],
                    key_buf[r, :, v * HD : (v + 1) * HD],
                    (((1,), (1,)), ((), ())),
                    preferred_element_type=jnp.float32,
                )
                for v in range(kv_count)
            ],
            axis=0,
        )
        scores = jnp.where(live, scores * score_scale, neg_large)
        high = jnp.max(scores, axis=1, keepdims=True)
        weights = jnp.where(live, jnp.exp(scores - high), 0.0)
        total = jnp.sum(weights, axis=1, keepdims=True)
        low = weights.astype(jnp.bfloat16)
        for v in range(kv_count):
            span = slice(v * group_size, (v + 1) * group_size)
            at = slice(r * group_size, (r + 1) * group_size)
            part_value[v, at, :] = jnp.dot(
                low[span],
                value_buf[r, :, v * HD : (v + 1) * HD],
                preferred_element_type=jnp.float32,
            )
            part_high[v, at, :] = jnp.broadcast_to(high[span], (group_size, HD))
            part_total[v, at, :] = jnp.broadcast_to(total[span], (group_size, HD))

    heads = rows * group_size
    square = lax.broadcasted_iota(jnp.int32, (heads, 128), 0) == lax.broadcasted_iota(
        jnp.int32, (heads, 128), 1
    )
    for v in range(kv_count):
        value_all[v] = part_value[v].astype(jnp.bfloat16)
        high_row = jnp.sum(jnp.where(square, part_high[v], 0.0), axis=0, keepdims=True)
        total_row = jnp.sum(jnp.where(square, part_total[v], 0.0), axis=0, keepdims=True)
        stat_all[v] = jnp.concatenate(
            [high_row, total_row, jnp.zeros((6, 128), jnp.float32)], axis=0
        )
    part_sends = []
    for d in t_offsets:
        dest = t_at(d)
        part_sends.append(
            remote("tensor", d, 1, value_all.at[dest], value_all.at[kv_count + t_me])
        )
        part_sends.append(remote("tensor", d, 2, stat_all.at[dest], stat_all.at[kv_count + t_me]))
    for copy in part_sends:
        copy.start()

    mine = t_me * HD
    own_key = new_key_ref[:, pl.ds(pl.multiple_of(mine, HD), HD)].astype(jnp.float32)
    own_value = new_value_ref[:, pl.ds(pl.multiple_of(mine, HD), HD)].astype(jnp.float32)

    def spread(block):
        wide_block = jnp.broadcast_to(block[:, None, :], (rows, group_size, HD))
        return wide_block.reshape(heads, HD)

    my_query = jnp.concatenate(
        [
            query_heads[pl.ds(t_me * heads + r, group_size, stride=rows), :]
            for r in range(rows)
        ],
        axis=0,
    )
    own_score = jnp.sum(my_query * spread(own_key), axis=1, keepdims=True) * score_scale
    for copy in part_sends:
        copy.wait_recv()
    highs, totals, values = [], [], []
    for s in range(tensor_count):
        at = jnp.where(s == 0, t_me, kv_count + t_at(-s))
        stats = stat_all[at]
        highs.append(
            jnp.sum(
                jnp.where(square, jnp.broadcast_to(stats[0:1], (heads, 128)), 0.0),
                axis=1,
                keepdims=True,
            )
        )
        totals.append(
            jnp.sum(
                jnp.where(square, jnp.broadcast_to(stats[1:2], (heads, 128)), 0.0),
                axis=1,
                keepdims=True,
            )
        )
        values.append(value_all[at].astype(jnp.float32))
    highest = own_score
    for high in highs:
        highest = jnp.maximum(highest, high)
    own_weight = jnp.exp(own_score - highest)
    total = own_weight
    numerator = own_weight.astype(jnp.bfloat16).astype(jnp.float32) * spread(own_value)
    for high, part, value in zip(highs, totals, values):
        factor = jnp.exp(high - highest)
        total = total + factor * part
        numerator = numerator + factor * value
    attended = (numerator / total).astype(jnp.bfloat16)
    to_row = lax.broadcasted_iota(jnp.int32, (heads, heads), 0)
    from_row = lax.broadcasted_iota(jnp.int32, (heads, heads), 1)
    swap = (from_row == (to_row % rows) * group_size + to_row // rows).astype(jnp.bfloat16)
    by_head = jnp.dot(swap, attended, preferred_element_type=jnp.float32)
    attended = jnp.concatenate(
        [by_head[h * rows : (h + 1) * rows] for h in range(group_size)], axis=1
    ).astype(jnp.bfloat16)

    proj_copy.wait()

    def stack(block):
        return jnp.concatenate([block[:, :half], block[:, half:]], axis=0).astype(jnp.bfloat16)

    def unstack(block):
        block = block.astype(jnp.float32)
        return jnp.concatenate([block[:rows], block[rows:]], axis=1)

    term_sends = []
    for d in list(t_offsets) + [tensor_count]:
        dest = t_at(d % tensor_count)
        term = jnp.dot(
            attended,
            proj_buf[:, pl.ds(pl.multiple_of(dest * width, width), width)],
            preferred_element_type=jnp.float32,
        )
        if d < tensor_count:
            term_all[tensor_count + d] = stack(term)
            copy = remote(
                "tensor", d, 3, term_all.at[tensor_count + d], term_all.at[t_me]
            )
            copy.start()
            term_sends.append(copy)
        else:
            term_all[t_me] = stack(term)
    for copy in term_sends:
        copy.wait_recv()
    proj_sum = unstack(term_all[0])
    for s in range(1, tensor_count):
        proj_sum = proj_sum + unstack(term_all[s])
    residual = (hidden_ref[...].astype(jnp.float32) + proj_sum).astype(jnp.bfloat16)
    wide = residual.astype(jnp.float32)
    rows_all[e_me] = stack(wide * gain_ref[...].astype(jnp.float32).reshape(1, width))
    square_all[e_me] = jnp.where(
        lane == e_me * rows + row, jnp.sum(wide * wide, axis=1, keepdims=True), 0.0
    )
    row_sends = []
    for d in e_offsets:
        row_sends.append(remote("expert", d, 4, rows_all.at[e_me], rows_all.at[e_me]))
        row_sends.append(remote("expert", d, 5, square_all.at[e_me], square_all.at[e_me]))
    for copy in row_sends:
        copy.start()

    for copy in info_sends:
        copy.wait_recv()
    all_rows = owner_count * rows
    slot_total = experts * slots
    info = jnp.concatenate([info_all[b] for b in range(owner_count)], axis=0)

    def picker(shape, slot_dim):
        slot = lax.broadcasted_iota(jnp.int32, shape, slot_dim)
        other = lax.broadcasted_iota(jnp.int32, shape, 1 - slot_dim)
        wanted = e_me * (experts * MOST) + (slot // slots) * MOST + slot % MOST
        return jnp.where(other == wanted, 1.0, 0.0)

    def same_block(shape, slot_dim):
        slot = lax.broadcasted_iota(jnp.int32, shape, slot_dim)
        other = lax.broadcasted_iota(jnp.int32, shape, 1 - slot_dim)
        return (slot // MOST) % owner_count == other // rows

    by_slot = lax.dot_general(
        picker((slot_total, 128), 0),
        info,
        (((1,), (1,)), ((), ())),
        precision=lax.Precision.HIGHEST,
        preferred_element_type=jnp.float32,
    )
    placing = jnp.where(same_block((slot_total, all_rows), 0) & (by_slot > 0.0), 1.0, 0.0)
    by_row = lax.dot_general(
        info,
        picker((slot_total, 128), 0),
        (((1,), (1,)), ((), ())),
        precision=lax.Precision.HIGHEST,
        preferred_element_type=jnp.float32,
    )
    by_row = jnp.where(same_block((all_rows, slot_total), 1), by_row, 0.0)
    gate_high = by_row.astype(jnp.bfloat16)
    gate_low = (by_row - gate_high.astype(jnp.float32)).astype(jnp.bfloat16)

    for copy in row_sends:
        copy.wait_recv()
    gathered = jnp.concatenate([unstack(rows_all[b]) for b in range(owner_count)], axis=0)
    slot_rows[...] = jnp.dot(
        placing.astype(jnp.bfloat16),
        gathered.astype(jnp.bfloat16),
        preferred_element_type=jnp.float32,
    ).astype(jnp.bfloat16)
    squares = square_all[0]
    for b in range(1, owner_count):
        squares = squares + square_all[b]
    square_sum[t_me] = squares
    square_sends = [
        remote("tensor", d, 6, square_sum.at[t_me], square_sum.at[t_me]) for d in t_offsets
    ]
    for copy in square_sends:
        copy.start()

    def pre_copy(i):
        d, k = lax.rem(i, tensor_count), i // tensor_count
        return pltpu.make_async_remote_copy(
            src_ref=pre_mine.at[i],
            dst_ref=pre_got.at[k, d],
            send_sem=pre_send.at[k, d],
            recv_sem=pre_recv.at[k, d],
            device_id={"tensor": t_at(1 + d)},
            device_id_type=pl.DeviceIdType.MESH,
        )

    def hid_copy(k, d):
        pair = t_me * per_owner + k
        return pltpu.make_async_remote_copy(
            src_ref=hidden_all.at[pair],
            dst_ref=hidden_all.at[pair],
            send_sem=hid_send.at[k, d - 1],
            recv_sem=hid_recv.at[k, d - 1],
            device_id={"tensor": t_at(d)},
            device_id_type=pl.DeviceIdType.MESH,
        )

    def reduce_pair(k):
        own = k * tensor_count + tensor_count - 1
        total = pre_mine[own].astype(jnp.float32)
        for d in range(tensor_count - 1):
            pre_copy(k * tensor_count + d).wait_recv()
            total = total + pre_got[k, d].astype(jnp.float32)
        pair = t_me * per_owner + k
        scale = slot_scale[pl.ds(pl.multiple_of(pair * 2 * slots, 2 * slots), 2 * slots), 0:1]
        total = total * scale
        gate, up = total[:, :units], total[:, units:]
        hidden_all[pair] = (gate / (1.0 + jnp.exp(-gate)) * up).astype(jnp.bfloat16)
        for d in t_offsets:
            hid_copy(k, d).start()

    lag = 3

    def scale_slots():
        for copy in square_sends:
            copy.wait_recv()
        squares = square_sum[0]
        for s in range(1, tensor_count):
            squares = squares + square_sum[s]
        mean_square = jnp.sum(squares, axis=0, keepdims=True) / (width * tensor_count)
        scale = lax.rsqrt(mean_square + 1e-06)
        slot_scale[...] = jnp.broadcast_to(
            jnp.sum(placing * scale[:, :all_rows], axis=1, keepdims=True), (slot_total, 128)
        )

    def gate_step(i, carry):
        pair = gate_pair(i)
        slot = lax.rem(i, gate_slots)
        gate_copy(i).wait()
        block = slot_rows[pl.ds(pl.multiple_of(pair * 2 * slots, 2 * slots), 2 * slots), :]
        first = jnp.dot(block, gate_buf[slot, 0], preferred_element_type=jnp.float32)
        second = jnp.dot(block, gate_buf[slot, 1], preferred_element_type=jnp.float32)
        pre_mine[i] = jnp.concatenate([first[:slots], second[slots:]], axis=0).astype(
            jnp.bfloat16
        )

        @pl.when(lax.rem(i, tensor_count) < tensor_count - 1)
        def _():
            pre_copy(i).start()

        @pl.when(i + gate_slots < pairs)
        def _():
            gate_copy(i + gate_slots).start()

        @pl.when(i == lag)
        def _():
            scale_slots()

        @pl.when((i - lag >= tensor_count - 1) & (lax.rem(i - lag, tensor_count) == tensor_count - 1))
        def _():
            reduce_pair((i - lag) // tensor_count)

        return carry

    lax.fori_loop(0, pairs, gate_step, 0)

    def down_step(i, carry):
        pair = down_pair(i)
        slot = lax.rem(i, down_slots)
        d, k = lax.rem(i, tensor_count), i // tensor_count

        @pl.when(d > 0)
        def _():
            pltpu.make_async_remote_copy(
                src_ref=hidden_all.at[pair],
                dst_ref=hidden_all.at[pair],
                send_sem=hid_send.at[k, tensor_count - d - 1],
                recv_sem=hid_recv.at[k, tensor_count - d - 1],
                device_id={"tensor": t_at(d)},
                device_id_type=pl.DeviceIdType.MESH,
            ).wait_recv()

        down_copy(i).wait()
        block = hidden_all[pair]
        first = jnp.dot(block, down_buf[slot, 0], preferred_element_type=jnp.float32)
        second = jnp.dot(block, down_buf[slot, 1], preferred_element_type=jnp.float32)
        result_all[pl.ds(pl.multiple_of(pair * 2 * slots, 2 * slots), 2 * slots), :] = (
            jnp.concatenate([first[:slots], second[slots:]], axis=0).astype(jnp.bfloat16)
        )

        @pl.when(i + down_slots < pairs)
        def _():
            down_copy(i + down_slots).start()

        return carry

    last = (per_owner - 1) * tensor_count
    lax.fori_loop(0, last, down_step, 0)
    reduce_pair(per_owner - 1)
    lax.fori_loop(last, pairs, down_step, 0)

    both = jnp.dot(
        jnp.concatenate([gate_high, gate_low], axis=0),
        result_all[...],
        preferred_element_type=jnp.float32,
    )
    mixture = both[:all_rows] + both[all_rows:]
    for b in range(owner_count):
        mix_mine[b] = stack(mixture[b * rows : (b + 1) * rows])
    mix_sends = [
        remote("expert", d, 7, mix_mine.at[e_at(d)], mix_got.at[d - 1]) for d in e_offsets
    ]
    for copy in mix_sends:
        copy.start()
    for copy in mix_sends:
        copy.wait_recv()
    total = wide + unstack(mix_mine[e_me])
    for d in e_offsets:
        total = total + unstack(mix_got[d - 1])
    out_ref[...] = total.astype(jnp.bfloat16)

    for copy in info_sends + part_sends + term_sends + row_sends + square_sends + mix_sends:
        copy.wait_send()
    for k in range(per_owner):
        for d in range(tensor_count - 1):
            pre_copy(k * tensor_count + d).wait_send()
            hid_copy(k, d + 1).wait_send()


def fits_kernel(shapes, tensor_count, owner_count):
    queries, keys, gate_up, down_proj = shapes
    rows = queries[0]
    head_count = queries[1] // HD
    experts = gate_up[0]
    return (
        tensor_count == KV
        and rows == 8
        and head_count == 8 * KV
        and owner_count * MOST == 8
        and experts * owner_count * MOST == 128
        and experts % (2 * tensor_count) == 0
        and gate_up[1] % 256 == 0
        and down_proj[1] % 128 == 0
        and keys[1] % 128 == 0
    )


def fused(
    hidden_in,
    queries,
    cache_keys,
    cache_values,
    new_key,
    new_value,
    cache_lengths,
    out_weight,
    norm_gain,
    gate_probs,
    expert_ids,
    gate_up,
    down_proj,
):
    tensor_count = lax.axis_size("tensor")
    owner_count = lax.axis_size("expert")
    rows, width = hidden_in.shape
    group_size = queries.shape[1] // HD // KV
    experts, units = gate_up.shape[0], down_proj.shape[1]
    pairs = experts // 2
    per_owner = pairs // tensor_count
    slots = owner_count * MOST
    heads = rows * group_size
    half = width // 2
    vmem = pl.BlockSpec(memory_space=pltpu.VMEM)
    far = pl.BlockSpec(memory_space=pl.ANY)
    dma = pltpu.SemaphoreType.DMA
    f32, bf16 = jnp.float32, jnp.bfloat16
    gate_slots, down_slots = min(5, pairs), min(4, pairs)
    others = max(tensor_count, owner_count) - 1
    return pl.pallas_call(
        functools.partial(fused_kernel, tensor_count, owner_count),
        out_shape=jax.ShapeDtypeStruct((rows, width), bf16),
        in_specs=[vmem] * 4
        + [pl.BlockSpec(memory_space=pltpu.SMEM)]
        + [vmem] * 3
        + [far] * 5,
        out_specs=vmem,
        scratch_shapes=[
            pltpu.VMEM(cache_keys.shape, bf16),
            pltpu.VMEM(cache_values.shape, bf16),
            pltpu.VMEM(out_weight.shape, bf16),
            pltpu.VMEM((gate_slots, 2) + gate_up.shape[1:], bf16),
            pltpu.VMEM((down_slots, 2) + down_proj.shape[1:], bf16),
            pltpu.VMEM((KV * heads, HD), f32),
            pltpu.VMEM((KV, heads, HD), f32),
            pltpu.VMEM((KV, heads, HD), f32),
            pltpu.VMEM((KV, heads, HD), f32),
            pltpu.VMEM((KV + tensor_count, 8, 128), f32),
            pltpu.VMEM((KV + tensor_count, heads, HD), bf16),
            pltpu.VMEM((2 * tensor_count, 2 * rows, half), bf16),
            pltpu.VMEM((owner_count, rows, 128), f32),
            pltpu.VMEM((owner_count, 2 * rows, half), bf16),
            pltpu.VMEM((owner_count, rows, 128), f32),
            pltpu.VMEM((tensor_count, rows, 128), f32),
            pltpu.VMEM((experts * slots, width), bf16),
            pltpu.VMEM((experts * slots, 128), f32),
            pltpu.VMEM((pairs, 2 * slots, 2 * units), bf16),
            pltpu.VMEM((per_owner, tensor_count - 1, 2 * slots, 2 * units), bf16),
            pltpu.VMEM((pairs, 2 * slots, units), bf16),
            pltpu.VMEM((experts * slots, width), bf16),
            pltpu.VMEM((owner_count, 2 * rows, half), bf16),
            pltpu.VMEM((owner_count - 1, 2 * rows, half), bf16),
            dma((3,)),
            dma((gate_slots,)),
            dma((down_slots,)),
            dma((8, others)),
            dma((8, others)),
            dma((per_owner, tensor_count - 1)),
            dma((per_owner, tensor_count - 1)),
            dma((per_owner, tensor_count - 1)),
            dma((per_owner, tensor_count - 1)),
        ],
        compiler_params=pltpu.CompilerParams(
            collective_id=0, has_side_effects=True, vmem_limit_bytes=62 * 1024 * 1024
        ),
    )(
        hidden_in,
        queries,
        new_key,
        new_value,
        cache_lengths,
        norm_gain,
        gate_probs,
        expert_ids,
        cache_keys,
        cache_values,
        out_weight,
        gate_up,
        down_proj,
    )


def layer(*args):
    shapes = (args[1].shape, args[2].shape, args[11].shape, args[12].shape)
    if fits_kernel(shapes, lax.axis_size("tensor"), lax.axis_size("expert")):
        return fused(*args)
    return body(*args)


def solution(mesh):
    return jax.shard_map(
        layer,
        mesh=mesh,
        in_specs=(
            P(("groups", "expert"), "tensor"),
            P(("groups", "expert"), None),
            P(("groups", "expert"), "tensor", None),
            P(("groups", "expert"), "tensor", None),
            P(("groups", "expert"), None),
            P(("groups", "expert"), None),
            P(("groups", "expert")),
            P("tensor", None),
            P("tensor"),
            P(("groups", "expert"), None),
            P(("groups", "expert"), None),
            P("expert", "tensor", None),
            P("expert", None, "tensor"),
        ),
        out_specs=P(("groups", "expert"), "tensor"),
        check_vma=False,
    )
```
